32 devices in a mesh: groups: 2 (over y), sink: 16 (over z, x, core).
Axes of the slice: x: 2, y: 2, z: 4, core: 2. Of those that a mesh axis runs over, the one named last changes fastest.
Arguments:
- eigvecs: bfloat16 [16, 2, 3, 192, 8192], P('groups', None, None, None, 'sink'), parts along dimension 0
- momentum: int32 [6], P('groups'), parts along dimension 0, may hold values from -5 to 5, as said below
- peram: bfloat16 [32, 2, 768, 768], P(('groups', 'sink')), parts along dimension 0, may hold values from -0.009338379 to 0.009338379
- times: int32 [32, 2], P(('groups', 'sink')), parts along dimension 0, may hold values from 0 to 7, as said below
Outputs:
- blocks: bfloat16 [32, 2, 768, 768], P(('groups', 'sink')), parts along dimension 0
The draws below stay inside these ranges and needn't reach their ends.
There are 2 independent parts, one for each index of `groups`. The reference program is written for one: setup_inputs(seed, part) draws one part's arguments, and reference() takes and returns one part's arrays. A program takes and returns all parts, laid end to end along the dimension named above; each array names one. Nothing has to cross between parts.
Inputs may be any that keep to these rules, and one draw needn't show every extreme that they name: `momentum`: the three components are distinct; one is -5 and one is 5. In each of the two columns every timeslice appears exactly 16 // 8 times.
All inputs are finite; a program needn't handle non-finite values.
Results may differ from the reference program's by a relative error of at most 0.0075.
Values may be sent and summed in bfloat16 or wider, within the bound.
No kernel may reach another device: no remote copies, remote signals or barrier semaphores. Data moves between devices by JAX's collectives and lax.ppermute only.
A program may use at most 64 MiB of HBM per device.

```python
import math
import jax
import jax.numpy as jnp
from jax import lax

K = 192
NT = 8
SITES_DEV = 512
SITES = 8192
PAIRS = 16
N_SINK = 16


def draw_eigvecs(key, part):
    shape = (NT, 2, 3, K, SITES)
    base = jax.random.normal(key, shape, jnp.float32)
    count = SITES // SITES_DEV
    device = (jnp.arange(SITES, dtype=jnp.int32) // SITES_DEV).astype(jnp.float32)
    ramp = 0.6 + 0.9 * device / (count - 1)
    return (base * ramp * (3.0 * SITES) ** (-0.25)).astype(jnp.bfloat16)


def draw_momentum(key, part):
    middle = jax.random.randint(jax.random.fold_in(key, 7), (1,), -4, 5, dtype=jnp.int32)
    triple = jnp.concatenate([jnp.array([-5, 5], jnp.int32), middle])
    return jax.random.permutation(jax.random.fold_in(key, 8), triple).astype(jnp.int32)


def draw_times(key, part):
    order = jnp.arange(PAIRS, dtype=jnp.int32) % NT
    first = jax.random.permutation(jax.random.fold_in(key, 1), order)
    second = jax.random.permutation(jax.random.fold_in(key, 2), order)
    return jnp.stack([first, second], axis=1).astype(jnp.int32)


def block_scale(stream_key, shape, pieces, smallest, largest):
    def one(axis_at, blocks):
        steps = jax.random.uniform(jax.random.fold_in(jax.random.fold_in(stream_key, 6), axis_at), (blocks,), jnp.float32, smallest / len(pieces), largest / len(pieces))
        return jnp.repeat(jnp.exp(steps), shape[axis_at] // blocks).reshape((-1,) + (1,) * (len(shape) - axis_at - 1))

    factor_of = one(*pieces[0])
    for cut in pieces[1:]:
        factor_of = factor_of * one(*cut)
    return factor_of


def noise(rng, dims, scale, limit, pieces=(), kind=jnp.bfloat16):
    loudness = block_scale(rng, dims, pieces, -0.22, 0.18) if pieces else 1.0
    result = jax.random.normal(rng, dims, jnp.float32) * scale * loudness
    return jnp.minimum(jnp.maximum(result, -limit), limit).astype(kind)


def setup_inputs(seed: int = 0, part: int = 0) -> dict:
    seeds = jax.random.split(jax.random.key(seed), 5)
    own_keys = jax.random.split(jax.random.fold_in(seeds[4], part), 5)
    return {
        "eigvecs": draw_eigvecs(jax.random.fold_in(jax.random.fold_in(seeds[4], part), 71), part),
        "momentum": draw_momentum(jax.random.fold_in(jax.random.fold_in(seeds[4], part), 71), part),
        "peram": noise(own_keys[2], (PAIRS, 2, 4 * K, 4 * K), (0.3 / K), 0.009338379, ((0, 16),)),
        "times": draw_times(jax.random.fold_in(jax.random.fold_in(seeds[4], part), 71), part),
    }


def angles(momentum):
    site = jnp.arange(SITES_DEV * N_SINK, dtype=jnp.int32)
    first = site // SITES_DEV
    local = site % SITES_DEV
    second = local // 16
    third = local % 16
    extent = SITES_DEV // 16
    frac = jnp.mod(momentum[0] * first, N_SINK).astype(jnp.float32) / N_SINK
    frac = frac + jnp.mod(momentum[1] * second, extent).astype(jnp.float32) / extent
    frac = frac + jnp.mod(momentum[2] * third, 16).astype(jnp.float32) / 16.0
    return (2.0 * math.pi) * frac


def rounded(value):
    return lax.optimization_barrier(value.astype(jnp.bfloat16)).astype(jnp.float32)


def slice_elemental(vectors, cosine, sine):
    vec_re = vectors[0].astype(jnp.float32)
    vec_im = vectors[1].astype(jnp.float32)
    rot_re = rounded(cosine * vec_re + sine * vec_im)
    rot_im = rounded(cosine * vec_im - sine * vec_re)
    real = jnp.einsum("ckx,clx->kl", vec_re, rot_re) + jnp.einsum("ckx,clx->kl", vec_im, rot_im)
    imag = jnp.einsum("ckx,clx->kl", vec_re, rot_im) - jnp.einsum("ckx,clx->kl", vec_im, rot_re)
    return jnp.concatenate([real, imag], axis=-1)


def reference(eigvecs, momentum, peram, times):
    theta = angles(momentum)
    cosine = jnp.cos(theta)
    sine = jnp.sin(theta)
    partial_sums = lax.map(lambda vectors: slice_elemental(vectors, cosine, sine), eigvecs)
    elemental = partial_sums.astype(jnp.bfloat16)
    signs = jnp.array([1.0, 1.0, -1.0, -1.0], jnp.float32)

    def one_pair(item):
        block, pair = item
        sink_el = elemental[pair[0]].astype(jnp.float32)
        src_el = elemental[pair[1]].astype(jnp.float32)
        width = sink_el.shape[0]
        a_re = sink_el[:, :width]
        a_im = sink_el[:, width:]
        t_re = jnp.roll(block[0].astype(jnp.float32).reshape(4, width, 4 * width), 2, axis=0) * signs[:, None, None]
        t_im = jnp.roll(block[1].astype(jnp.float32).reshape(4, width, 4 * width), 2, axis=0) * signs[:, None, None]
        x_re = jnp.einsum("kl,alc->akc", a_re, t_re) - jnp.einsum("kl,alc->akc", a_im, t_im)
        x_im = jnp.einsum("kl,alc->akc", a_re, t_im) + jnp.einsum("kl,alc->akc", a_im, t_re)
        x_re = rounded(x_re.reshape(4 * width, 4 * width))
        x_im = rounded(x_im.reshape(4 * width, 4 * width))
        y_re = jnp.roll(x_re.reshape(4 * width, 4, width), 2, axis=1)
        y_im = jnp.roll(x_im.reshape(4 * width, 4, width), 2, axis=1)
        e_re = src_el[:, :width]
        e_im = src_el[:, width:]
        m_re = jnp.einsum("rbl,nl->rbn", y_re, e_re) + jnp.einsum("rbl,nl->rbn", y_im, e_im)
        m_im = jnp.einsum("rbl,nl->rbn", y_im, e_re) - jnp.einsum("rbl,nl->rbn", y_re, e_im)
        return jnp.stack([m_re.reshape(4 * width, 4 * width), m_im.reshape(4 * width, 4 * width)]).astype(jnp.bfloat16)

    return lax.map(one_pair, (peram, times))
```

```python
import functools
import math

import jax
import jax.numpy as jnp
from jax import lax
from jax.experimental import pallas as pl
from jax.experimental.pallas import tpu as pltpu
from jax.sharding import PartitionSpec as P

BF16 = jnp.bfloat16
F32 = jnp.float32
NT_DIMS = (((1,), (1,)), ((), ()))


def dot_nt(left, right):
    return lax.dot_general(left, right, NT_DIMS, preferred_element_type=F32)


def elemental_kernel(devices, scalars, vec, keep, send, trig, total):
    width, sites = vec.shape[3], vec.shape[4]

    @pl.when(pl.program_id(0) == 0)
    def _():
        local = lax.broadcasted_iota(jnp.int32, (8, sites), 1)
        extent = sites // 16
        turn = jnp.mod(scalars[0] * scalars[3], devices).astype(F32) / devices
        second = scalars[1] * lax.shift_right_logical(local, 4)
        turn = turn + jnp.mod(second, extent).astype(F32) / extent
        third = scalars[2] * jnp.bitwise_and(local, 15)
        turn = turn + jnp.mod(third, 16).astype(F32) / 16.0
        theta = (2.0 * math.pi) * turn
        trig[0] = jnp.cos(theta)
        trig[1] = jnp.sin(theta)

    cosine = trig[0, 0:1, :]
    sine = trig[1, 0:1, :]
    with_re = jnp.zeros((2 * width, width), F32)
    with_im = jnp.zeros((2 * width, width), F32)
    for color in range(vec.shape[2]):
        low_re = vec[0, 0, color]
        low_im = vec[0, 1, color]
        vec_re = low_re.astype(F32)
        vec_im = low_im.astype(F32)
        rot_re = (cosine * vec_re + sine * vec_im).astype(BF16)
        rot_im = (cosine * vec_im - sine * vec_re).astype(BF16)
        both = jnp.concatenate([low_re, low_im], axis=0)
        with_re = with_re + dot_nt(both, rot_re)
        with_im = with_im + dot_nt(both, rot_im)
    real = with_re[:width] + with_im[width:]
    imag = with_im[:width] - with_re[width:]
    total[...] = jnp.concatenate([real, imag], axis=1)
    rows = width // 4
    mine = jnp.bitwise_and(scalars[3], 3)
    for flip in range(4):
        start = pl.multiple_of(jnp.bitwise_xor(mine, flip) * rows, rows)
        block = total[pl.ds(start, rows), :]
        if flip % 2 == 0:
            keep[flip // 2, 0] = block
        else:
            send[flip // 2, 0] = block.astype(BF16)


def elementals(eigvecs, scalars, devices, first, count):
    _, _, colors, width, sites = eigvecs.shape
    rows = width // 4
    out_block = pl.BlockSpec((2, 1, rows, 2 * width), lambda t, s: (0, t, 0, 0))
    flops = count * 8 * colors * width * width * sites
    return pl.pallas_call(
        functools.partial(elemental_kernel, devices),
        grid_spec=pltpu.PrefetchScalarGridSpec(
            num_scalar_prefetch=1,
            grid=(count,),
            in_specs=[
                pl.BlockSpec((1, 2, colors, width, sites), lambda t, s: (first + t, 0, 0, 0, 0))
            ],
            out_specs=[out_block, out_block],
            scratch_shapes=[
                pltpu.VMEM((2, 8, sites), F32),
                pltpu.VMEM((width, 2 * width), F32),
            ],
        ),
        out_shape=[
            jax.ShapeDtypeStruct((2, count, rows, 2 * width), F32),
            jax.ShapeDtypeStruct((2, count, rows, 2 * width), BF16),
        ],
        compiler_params=pltpu.CompilerParams(vmem_limit_bytes=24 * 1024 * 1024),
        cost_estimate=pl.CostEstimate(
            flops=flops, bytes_accessed=count * 2 * colors * width * sites * 2, transcendentals=0
        ),
        name="partial_elementals",
    )(scalars, eigvecs)


def block_kernel(scalars, own, by_core, by_pair, by_both, peram, out, sink_el, src_el, left_mat, right_mat):
    width = sink_el.shape[0]
    rows = width // 4

    @pl.when(pl.program_id(0) == 0)
    def _():
        for flip, part in enumerate((own, by_core, by_pair, by_both)):
            start = pl.multiple_of(jnp.bitwise_xor(scalars[0], flip) * rows, rows)
            sink_el[pl.ds(start, rows), :] = part[0]
            src_el[pl.ds(start, rows), :] = part[1]
        a_re = sink_el[:, :width]
        a_im = sink_el[:, width:]
        left_mat[:width] = jnp.concatenate([a_re, -a_im], axis=1)
        left_mat[width:] = jnp.concatenate([a_im, a_re], axis=1)
        e_re = src_el[:, :width]
        e_im = src_el[:, width:]
        right_mat[:width] = jnp.concatenate([e_re, e_im], axis=1)
        right_mat[width:] = jnp.concatenate([-e_im, e_re], axis=1)

    sign = jnp.where(pl.program_id(0) < 2, 1.0, -1.0)
    stacked = jnp.concatenate([peram[0], peram[1]], axis=0)
    left = jnp.dot(left_mat[...], stacked, preferred_element_type=F32) * sign
    left = left.astype(BF16)
    y_re = jnp.concatenate([left[:width, b * width : (b + 1) * width] for b in (2, 3, 0, 1)], axis=0)
    y_im = jnp.concatenate([left[width:, b * width : (b + 1) * width] for b in (2, 3, 0, 1)], axis=0)
    y_both = jnp.concatenate([y_re, y_im], axis=1)
    m_re = dot_nt(y_both, right_mat[:width]).astype(BF16)
    m_im = dot_nt(y_both, right_mat[width:]).astype(BF16)
    out[0] = jnp.concatenate([m_re[b * width : (b + 1) * width] for b in range(4)], axis=1)
    out[1] = jnp.concatenate([m_im[b * width : (b + 1) * width] for b in range(4)], axis=1)


def pair_block(peram, place, parts):
    full = peram.shape[-1]
    width = full // 4
    part_spec = pl.BlockSpec((2, width // 4, 2 * width), lambda a, s: (0, 0, 0))
    return pl.pallas_call(
        block_kernel,
        grid_spec=pltpu.PrefetchScalarGridSpec(
            num_scalar_prefetch=1,
            grid=(4,),
            in_specs=[part_spec] * 4
            + [pl.BlockSpec((2, width, full), lambda a, s: (0, (a + 2) % 4, 0))],
            out_specs=pl.BlockSpec((2, width, full), lambda a, s: (0, a, 0)),
            scratch_shapes=[
                pltpu.VMEM((width, 2 * width), BF16),
                pltpu.VMEM((width, 2 * width), BF16),
                pltpu.VMEM((2 * width, 2 * width), BF16),
                pltpu.VMEM((2 * width, 2 * width), BF16),
            ],
        ),
        out_shape=jax.ShapeDtypeStruct(peram.shape, BF16),
        compiler_params=pltpu.CompilerParams(vmem_limit_bytes=24 * 1024 * 1024),
        cost_estimate=pl.CostEstimate(
            flops=2 * 8 * full * full * width, bytes_accessed=8 * full * full, transcendentals=0
        ),
        name="meson_block",
    )(place, *parts, peram)


def swap(value, flip, devices):
    return lax.ppermute(value, "sink", [(i, i ^ flip) for i in range(devices)])


def sum_and_share(keep, send, device, devices):
    _, count, rows, both = keep.shape
    owners = devices // 4
    group = device // 4
    over_core = keep + swap(send, 1, devices).astype(F32)
    over_pair = over_core[0] + swap(over_core[1].astype(BF16), 2, devices).astype(F32)
    cut = over_pair.reshape(owners, count * rows // owners, both)
    low = cut.astype(BF16)
    total = lax.dynamic_index_in_dim(cut, group, 0, keepdims=False)
    for flip in range(1, owners):
        piece = lax.dynamic_index_in_dim(low, group ^ flip, 0, keepdims=False)
        total = total + swap(piece, 4 * flip, devices).astype(F32)
    total = total.astype(BF16)
    shared = [total] + [swap(total, 4 * flip, devices) for flip in range(1, owners)]
    shared = jnp.stack(shared)
    shared = jnp.take(shared, jnp.arange(owners) ^ group, axis=0)
    return shared.reshape(count, rows, both)


def shards(eigvecs, momentum, peram, times):
    devices = lax.axis_size("sink")
    device = lax.axis_index("sink")
    slices = eigvecs.shape[0]
    scalars = jnp.concatenate([momentum, device[None].astype(jnp.int32)])
    wanted = [times, swap(times, 1, devices)]
    other = swap(jnp.stack(wanted), 2, devices)
    wanted = wanted + [other[0], other[1]]
    half = slices // 2
    chunks = []
    for first in (0, half):
        keep, send = elementals(eigvecs, scalars, devices, first, half)
        chunks.append(sum_and_share(keep, send, device, devices))
    quarter = jnp.concatenate(chunks, axis=0)
    place = jnp.bitwise_and(device, 3)[None].astype(jnp.int32)
    outputs = []
    for pair in range(peram.shape[0]):
        parts = []
        for flip in range(4):
            chosen = jnp.stack(
                [
                    lax.dynamic_index_in_dim(quarter, wanted[flip][pair, side], 0, keepdims=False)
                    for side in range(2)
                ]
            )
            parts.append(chosen if flip == 0 else swap(chosen, flip, devices))
        outputs.append(pair_block(peram[pair], place, parts))
    return jnp.stack(outputs)


def solution(mesh):
    in_specs = (
        P("groups", None, None, None, "sink"),
        P("groups"),
        P(("groups", "sink"), None, None, None),
        P(("groups", "sink"), None),
    )
    out_specs = P(("groups", "sink"), None, None, None)
    return jax.shard_map(shards, mesh=mesh, in_specs=in_specs, out_specs=out_specs, check_vma=False)
```

```python
import functools
import math

import jax
import jax.numpy as jnp
from jax import lax
from jax.experimental import pallas as pl
from jax.experimental.pallas import tpu as pltpu
from jax.sharding import PartitionSpec as P

BF16 = jnp.bfloat16
F32 = jnp.float32
NT_DIMS = (((1,), (1,)), ((), ()))


def dot_nt(left, right):
    return lax.dot_general(left, right, NT_DIMS, preferred_element_type=F32)


def elemental_kernel(devices, first, momentum, eigvecs, keep, send, vec, arrived):
    count, _, colors, width, sites = vec.shape
    rows = width // 4

    def load(at):
        return pltpu.make_async_copy(eigvecs.at[first + at], vec.at[at], arrived.at[at])

    for at in range(count):
        load(at).start()
    device = lax.axis_index("sink")
    core = jnp.bitwise_and(device, 1)
    chip = jnp.bitwise_and(lax.shift_right_logical(device, 1), 1)
    local = lax.broadcasted_iota(jnp.int32, (1, sites), 1)
    extent = sites // 16
    turn = jnp.mod(momentum[0:1, 0:1] * device, devices).astype(F32) / devices
    second = momentum[0:1, 1:2] * lax.shift_right_logical(local, 4)
    turn = turn + jnp.mod(second, extent).astype(F32) / extent
    third = momentum[0:1, 2:3] * jnp.bitwise_and(local, 15)
    turn = turn + jnp.mod(third, 16).astype(F32) / 16.0
    theta = (2.0 * math.pi) * turn
    cosine = jnp.cos(theta)
    sine = jnp.sin(theta)
    for at in range(count):
        load(at).wait()
        plain = []
        rotated = []
        for color in range(colors):
            low_re = vec[at, 0, color]
            low_im = vec[at, 1, color]
            vec_re = low_re.astype(F32)
            vec_im = low_im.astype(F32)
            rot_re = (cosine * vec_re + sine * vec_im).astype(BF16)
            rot_im = (cosine * vec_im - sine * vec_re).astype(BF16)
            plain.append(jnp.concatenate([low_re, low_im], axis=0))
            rotated.append(jnp.concatenate([rot_re, rot_im], axis=0))
        both = dot_nt(jnp.concatenate(plain, axis=1), jnp.concatenate(rotated, axis=1))
        real = both[:width, :width] + both[width:, width:]
        imag = both[:width, width:] - both[width:, :width]
        total = jnp.concatenate([real, imag], axis=1)
        for side in range(2):

            @pl.when(core == side)
            def _():
                for pair in range(2):
                    slot = jnp.bitwise_xor(chip, pair)
                    mine = (2 * pair + side) * rows
                    other = (2 * pair + 1 - side) * rows
                    keep[slot, at] = total[mine : mine + rows]
                    send[slot, at] = total[other : other + rows].astype(BF16)


def elementals(eigvecs, momentum, devices, first, count):
    _, _, colors, width, sites = eigvecs.shape
    rows = width // 4
    flops = count * 8 * colors * width * width * sites
    return pl.pallas_call(
        functools.partial(elemental_kernel, devices, first),
        in_specs=[pl.BlockSpec(memory_space=pltpu.VMEM), pl.BlockSpec(memory_space=pl.ANY)],
        out_specs=[pl.BlockSpec(memory_space=pltpu.VMEM)] * 2,
        scratch_shapes=[
            pltpu.VMEM((count, 2, colors, width, sites), BF16),
            pltpu.SemaphoreType.DMA((count,)),
        ],
        out_shape=[
            jax.ShapeDtypeStruct((2, count, rows, 2 * width), F32),
            jax.ShapeDtypeStruct((2, count, rows, 2 * width), BF16),
        ],
        compiler_params=pltpu.CompilerParams(vmem_limit_bytes=52 * 1024 * 1024),
        cost_estimate=pl.CostEstimate(
            flops=flops, bytes_accessed=count * 2 * colors * width * sites * 2, transcendentals=0
        ),
        name="partial_elementals",
    )(momentum, eigvecs)


def select_kernel(firsts, relative, *refs):
    wanted = refs[:4]
    blocks = refs[4 : 4 + len(firsts)]
    outs = refs[4 + len(firsts) : 8 + len(firsts)]
    held = refs[-1]
    group = lax.shift_right_logical(lax.axis_index("sink"), 2)
    for block, first in zip(blocks, firsts):
        count = block.shape[0]
        for at in range(count):
            place = jnp.bitwise_xor(first, group) * count + at if relative else first + at
            held[place] = block[at]
    for out, times in zip(outs, wanted):
        for pair in range(out.shape[0]):
            for side in range(2):
                out[pair, side] = held[times[pair, side]]


def select(blocks, firsts, relative, wanted, slices):
    pairs = wanted[0].shape[0]
    _, rows, both = blocks[0].shape
    shape = jax.ShapeDtypeStruct((pairs, 2, rows, both), BF16)
    return pl.pallas_call(
        functools.partial(select_kernel, firsts, relative),
        in_specs=[pl.BlockSpec(memory_space=pltpu.SMEM)] * 4
        + [pl.BlockSpec(memory_space=pltpu.VMEM)] * len(blocks),
        out_specs=[pl.BlockSpec(memory_space=pltpu.VMEM)] * 4,
        scratch_shapes=[pltpu.VMEM((slices, rows, both), BF16)],
        out_shape=[shape] * 4,
        compiler_params=pltpu.CompilerParams(vmem_limit_bytes=8 * 1024 * 1024),
        name="select_slices",
    )(*wanted, *blocks)


def block_kernel(own, by_core, by_pair, by_both, peram, out, sink_el, src_el, left_mat, right_mat):
    width = sink_el.shape[0]
    window = right_mat.shape[1] // 2
    rows = width // 4
    place = jnp.bitwise_and(lax.axis_index("sink"), 3)

    @pl.when(pl.program_id(1) == 0)
    def _():
        for flip, part in enumerate((own, by_core, by_pair, by_both)):
            start = pl.multiple_of(jnp.bitwise_xor(place, flip) * rows, rows)
            sink_el[pl.ds(start, rows), :] = part[0, 0]
            src_el[pl.ds(start, rows), :] = part[0, 1]
        a_re = sink_el[:, :width]
        a_im = sink_el[:, width:]
        left_mat[:width] = jnp.concatenate([a_re, -a_im], axis=1)
        left_mat[width:] = jnp.concatenate([a_im, a_re], axis=1)
        e_re = src_el[:, :width]
        e_im = src_el[:, width:]
        pad = jnp.zeros((width, window - width), BF16)
        hole = jnp.zeros((window - width, 2 * window), BF16)
        even_re = jnp.concatenate([e_re, pad, e_im, pad], axis=1)
        even_im = jnp.concatenate([-e_im, pad, e_re, pad], axis=1)
        odd_re = jnp.concatenate([pad, e_re, pad, e_im], axis=1)
        odd_im = jnp.concatenate([pad, -e_im, pad, e_re], axis=1)
        right_mat[0] = jnp.concatenate([even_re, hole, even_im, hole], axis=0)
        right_mat[1] = jnp.concatenate([hole, odd_re, hole, odd_im], axis=0)

    sign = jnp.where(pl.program_id(1) < 2, 1.0, -1.0)
    stacked = jnp.concatenate([peram[0, 0], peram[0, 1]], axis=0)
    left = jnp.dot(left_mat[...], stacked, preferred_element_type=F32) * sign
    left = left.astype(BF16)
    results = []
    for odd in range(2):
        starts = [b * width - odd * (window - width) for b in (2 + odd, odd)]
        y_re = jnp.concatenate([left[:width, at : at + window] for at in starts], axis=0)
        y_im = jnp.concatenate([left[width:, at : at + window] for at in starts], axis=0)
        results.append(dot_nt(jnp.concatenate([y_re, y_im], axis=1), right_mat[odd]))
    edge = 2 * width - window
    for half in range(2):
        for part in range(2):
            even = results[0][half * width : (half + 1) * width, part * window : (part + 1) * window]
            odd = results[1][half * width : (half + 1) * width, part * window : (part + 1) * window]
            first = 2 * half * width
            out[0, part, :, first : first + edge] = even[:, :edge].astype(BF16)
            middle = even[:, edge:] + odd[:, : window - edge]
            out[0, part, :, first + edge : first + window] = middle.astype(BF16)
            out[0, part, :, first + window : first + 2 * width] = odd[:, window - edge :].astype(BF16)


def pair_blocks(peram, parts):
    pairs, _, full, _ = peram.shape
    width = full // 4
    window = -(-width // 128) * 128
    part_spec = pl.BlockSpec((1, 2, width // 4, 2 * width), lambda p, a: (p, 0, 0, 0))
    return pl.pallas_call(
        block_kernel,
        grid=(pairs, 4),
        in_specs=[part_spec] * 4
        + [pl.BlockSpec((1, 2, width, full), lambda p, a: (p, 0, (a + 2) % 4, 0))],
        out_specs=pl.BlockSpec((1, 2, width, full), lambda p, a: (p, 0, a, 0)),
        scratch_shapes=[
            pltpu.VMEM((width, 2 * width), BF16),
            pltpu.VMEM((width, 2 * width), BF16),
            pltpu.VMEM((2 * width, 2 * width), BF16),
            pltpu.VMEM((2, 2 * window, 2 * window), BF16),
        ],
        out_shape=jax.ShapeDtypeStruct(peram.shape, BF16),
        compiler_params=pltpu.CompilerParams(vmem_limit_bytes=24 * 1024 * 1024),
        cost_estimate=pl.CostEstimate(
            flops=pairs * 16 * full * full * width, bytes_accessed=pairs * 8 * full * full, transcendentals=0
        ),
        name="meson_blocks",
    )(*parts, peram)


def swap(value, flip, devices):
    return lax.ppermute(value, "sink", [(i, i ^ flip) for i in range(devices)])


def sum_near(keep, send, devices):
    over_core = keep + swap(send, 1, devices).astype(F32)
    return over_core[0] + swap(over_core[1].astype(BF16), 2, devices).astype(F32)


def sum_far(near, group, devices):
    count, rows, both = near.shape
    owners = devices // 4
    cut = near.reshape(owners, count * rows // owners, both)
    low = cut.astype(BF16)
    total = lax.dynamic_index_in_dim(cut, group, 0, keepdims=False)
    for flip in range(1, owners):
        piece = lax.dynamic_index_in_dim(low, group ^ flip, 0, keepdims=False)
        total = total + swap(piece, 4 * flip, devices).astype(F32)
    total = total.astype(BF16)
    return [total] + [swap(total, 4 * flip, devices) for flip in range(1, owners)]


def shards(eigvecs, momentum, peram, times):
    devices = lax.axis_size("sink")
    device = lax.axis_index("sink")
    owners = devices // 4
    group = device // 4
    slices, _, _, width, _ = eigvecs.shape
    rows = width // 4
    momentum = momentum.reshape(1, 3)
    core_times = swap(times, 1, devices)
    other = swap(jnp.concatenate([times, core_times]), 2, devices)
    wanted = [times, core_times, other[: times.shape[0]], other[times.shape[0] :]]
    half = slices // 2
    near = []
    for first in (0, half):
        keep, send = elementals(eigvecs, momentum, devices, first, half)
        near.append(sum_near(keep, send, devices))
    shared = sum_far(jnp.concatenate(near), group, devices)
    if slices % owners == 0:
        shared = [block.reshape(-1, rows, 2 * width) for block in shared]
        parts = select(shared, list(range(owners)), True, wanted, slices)
    else:
        shared = jnp.take(jnp.stack(shared), jnp.arange(owners) ^ group, axis=0)
        parts = select([shared.reshape(slices, rows, 2 * width)], [0], False, wanted, slices)
    parts = [parts[0]] + [swap(parts[flip], flip, devices) for flip in range(1, 4)]
    return pair_blocks(peram, parts)


def solution(mesh):
    in_specs = (
        P("groups", None, None, None, "sink"),
        P("groups"),
        P(("groups", "sink"), None, None, None),
        P(("groups", "sink"), None),
    )
    out_specs = P(("groups", "sink"), None, None, None)
    return jax.shard_map(shards, mesh=mesh, in_specs=in_specs, out_specs=out_specs, check_vma=False)
```

```python
import functools
import math

import jax
import jax.numpy as jnp
from jax import lax
from jax.experimental import pallas as pl
from jax.experimental.pallas import tpu as pltpu
from jax.sharding import PartitionSpec as P

BF16 = jnp.bfloat16
F32 = jnp.float32
NT_DIMS = (((1,), (1,)), ((), ()))
CHUNKS = ((1, 3), (1, 3))


def dot_nt(left, right):
    return lax.dot_general(left, right, NT_DIMS, preferred_element_type=F32)


def elemental_kernel(devices, first, arrivals, momentum, eigvecs, before, keep, send, vec, total, arrived):
    del before
    count, _, colors, width, sites = vec.shape
    rows = width // 4

    def load(at):
        return pltpu.make_async_copy(eigvecs.at[first + at], vec.at[at], arrived.at[at])

    for at in range(count):
        load(at).start()
    device = lax.axis_index("sink")
    core = jnp.bitwise_and(device, 1)
    chip = jnp.bitwise_and(lax.shift_right_logical(device, 1), 1)
    local = lax.broadcasted_iota(jnp.int32, (1, sites), 1)
    extent = sites // 16
    turn = jnp.mod(momentum[0:1, 0:1] * device, devices).astype(F32) / devices
    second = momentum[0:1, 1:2] * lax.shift_right_logical(local, 4)
    turn = turn + jnp.mod(second, extent).astype(F32) / extent
    third = momentum[0:1, 2:3] * jnp.bitwise_and(local, 15)
    turn = turn + jnp.mod(third, 16).astype(F32) / 16.0
    theta = (2.0 * math.pi) * turn
    cosine = jnp.cos(theta)
    sine = jnp.sin(theta)
    waits = [start for start, many in arrivals for _ in range(many)]
    for at in range(count):
        for late in range(at, count):
            if waits[late] == at:
                load(late).wait()
        plain = []
        rotated = []
        for color in range(colors):
            low_re = vec[at, 0, color]
            low_im = vec[at, 1, color]
            vec_re = low_re.astype(F32)
            vec_im = low_im.astype(F32)
            rot_re = (cosine * vec_re + sine * vec_im).astype(BF16)
            rot_im = (cosine * vec_im - sine * vec_re).astype(BF16)
            plain.append(jnp.concatenate([low_re, low_im], axis=0))
            rotated.append(jnp.concatenate([rot_re, rot_im], axis=0))
        both = dot_nt(jnp.concatenate(plain, axis=1), jnp.concatenate(rotated, axis=1))
        real = both[:width, :width] + both[width:, width:]
        imag = both[:width, width:] - both[width:, :width]
        total[at] = jnp.concatenate([real, imag], axis=1)
    for side in range(2):

        @pl.when(core == side)
        def _():
            for at in range(count):
                for pair in range(2):
                    slot = jnp.bitwise_xor(chip, pair)
                    mine = (2 * pair + side) * rows
                    other = (2 * pair + 1 - side) * rows
                    keep[slot, at] = total[at, mine : mine + rows]
                    send[slot, at] = total[at, other : other + rows].astype(BF16)


def elementals(eigvecs, momentum, first, arrivals, before, devices):
    _, _, colors, width, sites = eigvecs.shape
    rows = width // 4
    count = sum(arrivals)
    arrivals = [(sum(arrivals[:at]), many) for at, many in enumerate(arrivals)]
    return pl.pallas_call(
        functools.partial(elemental_kernel, devices, first, arrivals),
        in_specs=[pl.BlockSpec(memory_space=pltpu.VMEM)] + [pl.BlockSpec(memory_space=pl.ANY)] * 2,
        out_specs=[pl.BlockSpec(memory_space=pltpu.VMEM)] * 2,
        scratch_shapes=[
            pltpu.VMEM((count, 2, colors, width, sites), BF16),
            pltpu.VMEM((count, width, 2 * width), F32),
            pltpu.SemaphoreType.DMA((count,)),
        ],
        out_shape=[
            jax.ShapeDtypeStruct((2, count, rows, 2 * width), F32),
            jax.ShapeDtypeStruct((2, count, rows, 2 * width), BF16),
        ],
        compiler_params=pltpu.CompilerParams(vmem_limit_bytes=50 * 1024 * 1024),
        cost_estimate=pl.CostEstimate(
            flops=count * 8 * colors * width * width * sites,
            bytes_accessed=count * 2 * colors * width * sites * 2,
            transcendentals=0,
        ),
        name="partial_elementals",
    )(momentum, eigvecs, before)


def select_kernel(places, owners, *refs):
    wanted = refs[:4]
    blocks = refs[4 : 4 + len(places)]
    outs = refs[4 + len(places) : 8 + len(places)]
    held = refs[-1]
    group = jnp.bitwise_and(lax.shift_right_logical(lax.axis_index("sink"), 2), owners - 1)
    for block, (first, flip) in zip(blocks, places):
        count = block.shape[0]
        for at in range(count):
            start = first if flip is None else first + jnp.bitwise_xor(group, flip) * count
            held[start + at] = block[at]
    for out, times in zip(outs, wanted):
        for pair in range(out.shape[0]):
            for side in range(2):
                out[pair, side] = held[times[pair, side]]


def select(blocks, places, owners, wanted, slices):
    pairs = wanted[0].shape[0]
    _, rows, both = blocks[0].shape
    shape = jax.ShapeDtypeStruct((pairs, 2, rows, both), BF16)
    return pl.pallas_call(
        functools.partial(select_kernel, places, owners),
        in_specs=[pl.BlockSpec(memory_space=pltpu.SMEM)] * 4
        + [pl.BlockSpec(memory_space=pltpu.VMEM)] * len(blocks),
        out_specs=[pl.BlockSpec(memory_space=pltpu.VMEM)] * 4,
        scratch_shapes=[pltpu.VMEM((slices, rows, both), BF16)],
        out_shape=[shape] * 4,
        compiler_params=pltpu.CompilerParams(vmem_limit_bytes=8 * 1024 * 1024),
        name="select_slices",
    )(*wanted, *blocks)


def block_kernel(own, by_core, by_pair, by_both, peram, out, sink_el, src_el, left_mat, right_mat):
    width = sink_el.shape[0]
    window = right_mat.shape[1] // 2
    rows = width // 4
    place = jnp.bitwise_and(lax.axis_index("sink"), 3)

    @pl.when(pl.program_id(1) == 0)
    def _():
        for flip, part in enumerate((own, by_core, by_pair, by_both)):
            start = pl.multiple_of(jnp.bitwise_xor(place, flip) * rows, rows)
            sink_el[pl.ds(start, rows), :] = part[0, 0]
            src_el[pl.ds(start, rows), :] = part[0, 1]
        a_re = sink_el[:, :width]
        a_im = sink_el[:, width:]
        left_mat[:width] = jnp.concatenate([a_re, -a_im], axis=1)
        left_mat[width:] = jnp.concatenate([a_im, a_re], axis=1)
        e_re = src_el[:, :width]
        e_im = src_el[:, width:]
        pad = jnp.zeros((width, window - width), BF16)
        hole = jnp.zeros((window - width, 2 * window), BF16)
        even_re = jnp.concatenate([e_re, pad, e_im, pad], axis=1)
        even_im = jnp.concatenate([-e_im, pad, e_re, pad], axis=1)
        odd_re = jnp.concatenate([pad, e_re, pad, e_im], axis=1)
        odd_im = jnp.concatenate([pad, -e_im, pad, e_re], axis=1)
        right_mat[0] = jnp.concatenate([even_re, hole, even_im, hole], axis=0)
        right_mat[1] = jnp.concatenate([hole, odd_re, hole, odd_im], axis=0)

    sign = jnp.where(pl.program_id(1) < 2, 1.0, -1.0)
    stacked = jnp.concatenate([peram[0, 0], peram[0, 1]], axis=0)
    left = jnp.dot(left_mat[...], stacked, preferred_element_type=F32) * sign
    left = left.astype(BF16)
    results = []
    for odd in range(2):
        starts = [b * width - odd * (window - width) for b in (2 + odd, odd)]
        y_re = jnp.concatenate([left[:width, at : at + window] for at in starts], axis=0)
        y_im = jnp.concatenate([left[width:, at : at + window] for at in starts], axis=0)
        results.append(dot_nt(jnp.concatenate([y_re, y_im], axis=1), right_mat[odd]))
    edge = 2 * width - window
    for half in range(2):
        for part in range(2):
            even = results[0][half * width : (half + 1) * width, part * window : (part + 1) * window]
            odd = results[1][half * width : (half + 1) * width, part * window : (part + 1) * window]
            first = 2 * half * width
            out[0, part, :, first : first + edge] = even[:, :edge].astype(BF16)
            middle = even[:, edge:] + odd[:, : window - edge]
            out[0, part, :, first + edge : first + window] = middle.astype(BF16)
            out[0, part, :, first + window : first + 2 * width] = odd[:, window - edge :].astype(BF16)


def pair_blocks(peram, parts):
    pairs, _, full, _ = peram.shape
    width = full // 4
    window = -(-width // 128) * 128
    part_spec = pl.BlockSpec((1, 2, width // 4, 2 * width), lambda p, a: (p, 0, 0, 0))
    return pl.pallas_call(
        block_kernel,
        grid=(pairs, 4),
        in_specs=[part_spec] * 4
        + [pl.BlockSpec((1, 2, width, full), lambda p, a: (p, 0, (a + 2) % 4, 0))],
        out_specs=pl.BlockSpec((1, 2, width, full), lambda p, a: (p, 0, a, 0)),
        scratch_shapes=[
            pltpu.VMEM((width, 2 * width), BF16),
            pltpu.VMEM((width, 2 * width), BF16),
            pltpu.VMEM((2 * width, 2 * width), BF16),
            pltpu.VMEM((2, 2 * window, 2 * window), BF16),
        ],
        out_shape=jax.ShapeDtypeStruct(peram.shape, BF16),
        compiler_params=pltpu.CompilerParams(vmem_limit_bytes=24 * 1024 * 1024),
        cost_estimate=pl.CostEstimate(
            flops=pairs * 16 * full * full * width, bytes_accessed=pairs * 8 * full * full, transcendentals=0
        ),
        name="meson_blocks",
    )(*parts, peram)


def swap(value, flip, devices):
    return lax.ppermute(value, "sink", [(i, i ^ flip) for i in range(devices)])


def sum_near(keep, send, devices):
    over_core = keep + swap(send, 1, devices).astype(F32)
    given = over_core[1].astype(BF16)
    return over_core[0] + swap(given, 2, devices).astype(F32), given


def sum_far(near, flip, group, devices):
    half = near.shape[0] // 2
    if 8 * flip == devices:
        return [(near + swap(near.astype(BF16), 4 * flip, devices).astype(F32)).astype(BF16)]
    cut = near.reshape(2, half, near.shape[1])
    bit = jnp.bitwise_and(lax.shift_right_logical(group, flip.bit_length() - 1), 1)
    kept = lax.dynamic_index_in_dim(cut, bit, 0, keepdims=False)
    given = lax.dynamic_index_in_dim(cut, 1 - bit, 0, keepdims=False).astype(BF16)
    kept = kept + swap(given, 4 * flip, devices).astype(F32)
    blocks = sum_far(kept, 2 * flip, group, devices)
    low = blocks[0] if len(blocks) == 1 else jnp.concatenate(blocks)
    other = swap(low, 4 * flip, devices)
    return blocks + [other[at * blocks[0].shape[0] : (at + 1) * blocks[0].shape[0]] for at in range(len(blocks))]


def shards(eigvecs, momentum, peram, times):
    devices = lax.axis_size("sink")
    group = lax.shift_right_logical(lax.axis_index("sink"), 2)
    owners = devices // 8
    slices, _, _, width, _ = eigvecs.shape
    rows = width // 4
    momentum = momentum.reshape(1, 3)
    blocks = []
    places = []
    first = 0
    before = momentum
    nears = []
    for chunk in CHUNKS:
        arrivals = [part * slices // 8 for part in chunk]
        keep, send = elementals(eigvecs, momentum, first, arrivals, before, devices)
        if nears:
            send, nears[-1] = lax.optimization_barrier((send, nears[-1]))
        near, before = sum_near(keep, send, devices)
        nears.append(near)
        first += sum(arrivals)
    late_times, nears[-1] = lax.optimization_barrier((times, nears[-1]))
    core_times = swap(late_times, 1, devices)
    other = swap(jnp.concatenate([late_times, core_times]), 2, devices)
    wanted = [times, core_times, other[: times.shape[0]], other[times.shape[0] :]]
    first = 0
    for near in nears:
        count = near.shape[0]
        shared = sum_far(near.reshape(-1, 2 * width), 1, group, devices)
        if count % owners == 0:
            blocks += [block.reshape(-1, rows, 2 * width) for block in shared]
            places += [(first, flip) for flip in range(owners)]
        else:
            shared = jnp.take(jnp.stack(shared), jnp.arange(owners) ^ (group & (owners - 1)), axis=0)
            blocks.append(shared.reshape(count, rows, 2 * width))
            places.append((first, None))
        first += count
    parts = select(blocks, places, owners, wanted, slices)
    parts = [parts[0]] + [swap(parts[flip], flip, devices) for flip in range(1, 4)]
    return pair_blocks(peram, parts)


def solution(mesh):
    in_specs = (
        P("groups", None, None, None, "sink"),
        P("groups"),
        P(("groups", "sink"), None, None, None),
        P(("groups", "sink"), None),
    )
    out_specs = P(("groups", "sink"), None, None, None)
    return jax.shard_map(shards, mesh=mesh, in_specs=in_specs, out_specs=out_specs, check_vma=False)
```

```python
import functools
import math

import jax
import jax.numpy as jnp
from jax import lax
from jax.experimental import pallas as pl
from jax.experimental.pallas import tpu as pltpu
from jax.sharding import PartitionSpec as P

BF16 = jnp.bfloat16
F32 = jnp.float32
NT_DIMS = (((1,), (1,)), ((), ()))
CHUNKS = (4, 4)
ARRIVALS = (1, 2, 5)


def dot_nt(left, right):
    return lax.dot_general(left, right, NT_DIMS, preferred_element_type=F32)


def elemental_kernel(devices, chunks, arrivals, momentum, eigvecs, *refs):
    outs = refs[:-3]
    vec, total, arrived = refs[-3:]
    count, _, colors, width, sites = vec.shape
    rows = width // 4

    def load(at):
        return pltpu.make_async_copy(eigvecs.at[at], vec.at[at], arrived.at[at])

    for at in range(count):
        load(at).start()
    device = lax.axis_index("sink")
    core = jnp.bitwise_and(device, 1)
    chip = jnp.bitwise_and(lax.shift_right_logical(device, 1), 1)
    local = lax.broadcasted_iota(jnp.int32, (1, sites), 1)
    extent = sites // 16
    turn = jnp.mod(momentum[0:1, 0:1] * device, devices).astype(F32) / devices
    second = momentum[0:1, 1:2] * lax.shift_right_logical(local, 4)
    turn = turn + jnp.mod(second, extent).astype(F32) / extent
    third = momentum[0:1, 2:3] * jnp.bitwise_and(local, 15)
    turn = turn + jnp.mod(third, 16).astype(F32) / 16.0
    theta = (2.0 * math.pi) * turn
    cosine = jnp.cos(theta)
    sine = jnp.sin(theta)
    waits = [start for start, many in arrivals for _ in range(many)]
    for at in range(count):
        for late in range(at, count):
            if waits[late] == at:
                load(late).wait()
        plain = []
        rotated = []
        for color in range(colors):
            low_re = vec[at, 0, color]
            low_im = vec[at, 1, color]
            vec_re = low_re.astype(F32)
            vec_im = low_im.astype(F32)
            rot_re = (cosine * vec_re + sine * vec_im).astype(BF16)
            rot_im = (cosine * vec_im - sine * vec_re).astype(BF16)
            plain.append(jnp.concatenate([low_re, low_im], axis=0))
            rotated.append(jnp.concatenate([rot_re, rot_im], axis=0))
        both = dot_nt(jnp.concatenate(plain, axis=1), jnp.concatenate(rotated, axis=1))
        real = both[:width, :width] + both[width:, width:]
        imag = both[:width, width:] - both[width:, :width]
        total[at] = jnp.concatenate([real, imag], axis=1)
    for side in range(2):

        @pl.when(core == side)
        def _():
            first = 0
            for chunk, many in enumerate(chunks):
                keep, send = outs[2 * chunk : 2 * chunk + 2]
                for at in range(many):
                    for pair in range(2):
                        slot = jnp.bitwise_xor(chip, pair)
                        mine = (2 * pair + side) * rows
                        other = (2 * pair + 1 - side) * rows
                        keep[slot, at] = total[first + at, mine : mine + rows]
                        send[slot, at] = total[first + at, other : other + rows].astype(BF16)
                first += many


def elementals(eigvecs, momentum, devices):
    slices, _, colors, width, sites = eigvecs.shape
    rows = width // 4
    chunks = [part * slices // 8 for part in CHUNKS]
    arrivals = [part * slices // 8 for part in ARRIVALS]
    arrivals = [(sum(arrivals[:at]), many) for at, many in enumerate(arrivals)]
    shapes = []
    for count in chunks:
        shapes += [
            jax.ShapeDtypeStruct((2, count, rows, 2 * width), F32),
            jax.ShapeDtypeStruct((2, count, rows, 2 * width), BF16),
        ]
    outs = pl.pallas_call(
        functools.partial(elemental_kernel, devices, chunks, arrivals),
        in_specs=[pl.BlockSpec(memory_space=pltpu.VMEM), pl.BlockSpec(memory_space=pl.ANY)],
        out_specs=[pl.BlockSpec(memory_space=pltpu.VMEM)] * len(shapes),
        scratch_shapes=[
            pltpu.VMEM((slices, 2, colors, width, sites), BF16),
            pltpu.VMEM((slices, width, 2 * width), F32),
            pltpu.SemaphoreType.DMA((slices,)),
        ],
        out_shape=shapes,
        compiler_params=pltpu.CompilerParams(vmem_limit_bytes=50 * 1024 * 1024),
        cost_estimate=pl.CostEstimate(
            flops=slices * 8 * colors * width * width * sites,
            bytes_accessed=slices * 2 * colors * width * sites * 2,
            transcendentals=0,
        ),
        name="partial_elementals",
    )(momentum, eigvecs)
    return [outs[at : at + 2] for at in range(0, len(outs), 2)]


def select_kernel(firsts, *refs):
    many = sum(2 if halves else 1 for _, halves in firsts)
    wanted = refs[:4]
    blocks = refs[4 : 4 + many]
    outs = refs[4 + many : 12 + many]
    held = refs[-1]
    rows = held.shape[1]
    upper = jnp.bitwise_and(lax.shift_right_logical(lax.axis_index("sink"), 2), 1)
    for side in range(2):

        @pl.when(upper == side)
        def _():
            at = 0
            for first, halves in firsts:
                for flip in range(2 if halves else 1):
                    block = blocks[at]
                    start = (side ^ flip) * (rows // 2) if halves else 0
                    held[first : first + block.shape[0], start : start + block.shape[1], :] = block[...]
                    at += 1

    for at, times in enumerate(wanted):
        for side in range(2):
            out = outs[4 * side + at]
            for pair in range(out.shape[0]):
                out[pair] = held[times[pair, side]]


def select(blocks, firsts, wanted, slices, rows):
    pairs = wanted[0].shape[0]
    both = blocks[0].shape[2]
    shape = jax.ShapeDtypeStruct((pairs, rows, both), BF16)
    return pl.pallas_call(
        functools.partial(select_kernel, firsts),
        in_specs=[pl.BlockSpec(memory_space=pltpu.SMEM)] * 4
        + [pl.BlockSpec(memory_space=pltpu.VMEM)] * len(blocks),
        out_specs=[pl.BlockSpec(memory_space=pltpu.VMEM)] * 8,
        scratch_shapes=[pltpu.VMEM((slices, rows, both), BF16)],
        out_shape=[shape] * 8,
        compiler_params=pltpu.CompilerParams(vmem_limit_bytes=8 * 1024 * 1024),
        name="select_slices",
    )(*wanted, *blocks)


def gather_rows(pair, parts, full):
    rows = full.shape[0] // 4
    place = jnp.bitwise_and(lax.axis_index("sink"), 3)
    for flip, part in enumerate(parts):
        start = pl.multiple_of(jnp.bitwise_xor(place, flip) * rows, rows)
        full[pl.ds(start, rows), :] = part[pair]


def left_kernel(own, by_core, by_pair, by_both, peram, left, sink_el, left_mat):
    width = sink_el.shape[0]
    for pair in range(peram.shape[0]):
        gather_rows(pair, (own, by_core, by_pair, by_both), sink_el)
        a_re = sink_el[:, :width]
        a_im = sink_el[:, width:]
        left_mat[:width] = jnp.concatenate([a_re, -a_im], axis=1)
        left_mat[width:] = jnp.concatenate([a_im, a_re], axis=1)
        for a in range(4):
            band = slice((a + 2) % 4 * width, ((a + 2) % 4 + 1) * width)
            stacked = jnp.concatenate([peram[pair, 0, band], peram[pair, 1, band]], axis=0)
            both = jnp.dot(left_mat[...], stacked, preferred_element_type=F32)
            both = (both if a < 2 else -both).astype(BF16)
            left[pair, 0, a * width : (a + 1) * width] = both[:width]
            left[pair, 1, a * width : (a + 1) * width] = both[width:]


def right_kernel(own, by_core, by_pair, by_both, left, out, src_el, right_mat, block, stored):
    width = src_el.shape[0]
    window = right_mat.shape[1] // 2
    edge = 2 * width - window

    def store(pair, a):
        band = pl.ds(a * width, width)
        return pltpu.make_async_copy(block.at[a], out.at[pair, :, band, :], stored.at[a])

    for pair in range(left.shape[0]):
        gather_rows(pair, (own, by_core, by_pair, by_both), src_el)
        e_re = src_el[:, :width]
        e_im = src_el[:, width:]
        pad = jnp.zeros((width, window - width), BF16)
        hole = jnp.zeros((window - width, 2 * window), BF16)
        even_re = jnp.concatenate([e_re, pad, e_im, pad], axis=1)
        even_im = jnp.concatenate([-e_im, pad, e_re, pad], axis=1)
        odd_re = jnp.concatenate([pad, e_re, pad, e_im], axis=1)
        odd_im = jnp.concatenate([pad, -e_im, pad, e_re], axis=1)
        right_mat[0] = jnp.concatenate([even_re, hole, even_im, hole], axis=0)
        right_mat[1] = jnp.concatenate([hole, odd_re, hole, odd_im], axis=0)
        for a in range(4):
            band = slice(a * width, (a + 1) * width)
            results = []
            for odd in range(2):
                starts = [b * width - odd * (window - width) for b in (2 + odd, odd)]
                y_re = jnp.concatenate([left[pair, 0, band, at : at + window] for at in starts], axis=0)
                y_im = jnp.concatenate([left[pair, 1, band, at : at + window] for at in starts], axis=0)
                results.append(dot_nt(jnp.concatenate([y_re, y_im], axis=1), right_mat[odd]))
            if pair > 0:
                store(pair - 1, a).wait()
            for half in range(2):
                for part in range(2):
                    rect = slice(half * width, (half + 1) * width), slice(part * window, (part + 1) * window)
                    even = results[0][rect]
                    odd = results[1][rect]
                    first = 2 * half * width
                    block[a, part, :, first : first + edge] = even[:, :edge].astype(BF16)
                    middle = even[:, edge:] + odd[:, : window - edge]
                    block[a, part, :, first + edge : first + window] = middle.astype(BF16)
                    block[a, part, :, first + window : first + 2 * width] = odd[:, window - edge :].astype(BF16)
            store(pair, a).start()
    for a in range(4):
        store(left.shape[0] - 1, a).wait()


def pair_blocks(peram, sink_parts, src_parts):
    pairs, _, full, _ = peram.shape
    width = full // 4
    window = -(-width // 128) * 128
    params = pltpu.CompilerParams(vmem_limit_bytes=16 * 1024 * 1024)
    cost = pl.CostEstimate(
        flops=pairs * 8 * full * full * width, bytes_accessed=pairs * 4 * full * full, transcendentals=0
    )
    left = pl.pallas_call(
        left_kernel,
        in_specs=[pl.BlockSpec(memory_space=pltpu.VMEM)] * 5,
        out_specs=pl.BlockSpec(memory_space=pltpu.VMEM),
        scratch_shapes=[
            pltpu.VMEM((width, 2 * width), BF16),
            pltpu.VMEM((2 * width, 2 * width), BF16),
        ],
        out_shape=jax.ShapeDtypeStruct(peram.shape, BF16),
        compiler_params=params,
        cost_estimate=cost,
        name="left_product",
    )(*sink_parts, peram)
    return pl.pallas_call(
        right_kernel,
        in_specs=[pl.BlockSpec(memory_space=pltpu.VMEM)] * 5,
        out_specs=pl.BlockSpec(memory_space=pl.ANY),
        scratch_shapes=[
            pltpu.VMEM((width, 2 * width), BF16),
            pltpu.VMEM((2, 2 * window, 2 * window), BF16),
            pltpu.VMEM((4, 2, width, full), BF16),
            pltpu.SemaphoreType.DMA((4,)),
        ],
        out_shape=jax.ShapeDtypeStruct(peram.shape, BF16),
        compiler_params=params,
        cost_estimate=cost,
        name="meson_blocks",
    )(*src_parts, left)


def swap(value, flip, devices):
    return lax.ppermute(value, "sink", [(i, i ^ flip) for i in range(devices)])


def sum_near(keep, send, devices):
    over_core = keep + swap(send, 1, devices).astype(F32)
    return over_core[0] + swap(over_core[1].astype(BF16), 2, devices).astype(F32)


def sum_far(near, flip, group, devices):
    count, rows, both = near.shape
    if 8 * flip == devices:
        return [(near + swap(near.astype(BF16), 4 * flip, devices).astype(F32)).astype(BF16)]
    cut = near.reshape(count, 2, rows // 2, both)
    bit = jnp.bitwise_and(lax.shift_right_logical(group, flip.bit_length() - 1), 1)
    kept = lax.dynamic_index_in_dim(cut, bit, 1, keepdims=False)
    given = lax.dynamic_index_in_dim(cut, 1 - bit, 1, keepdims=False).astype(BF16)
    kept = kept + swap(given, 4 * flip, devices).astype(F32)
    blocks = sum_far(kept, 2 * flip, group, devices)
    if len(blocks) == 1:
        return blocks + [swap(blocks[0], 4 * flip, devices)]
    other = swap(jnp.stack(blocks), 4 * flip, devices)
    return [block for at in range(len(blocks)) for block in (blocks[at], other[at])]


def shards(eigvecs, momentum, peram, times):
    devices = lax.axis_size("sink")
    group = lax.shift_right_logical(lax.axis_index("sink"), 2)
    owners = devices // 8
    slices, _, _, width, _ = eigvecs.shape
    rows = width // 4
    momentum = momentum.reshape(1, 3)
    blocks = []
    firsts = []
    nears = [sum_near(keep, send, devices) for keep, send in elementals(eigvecs, momentum, devices)]
    first = 0
    for near in nears:
        count = near.shape[0]
        shared = sum_far(near, 1, group, devices)
        if first == 0:
            late_times, shared[0] = lax.optimization_barrier((times, shared[0]))
            core_times = swap(late_times, 1, devices)
            other = swap(jnp.concatenate([late_times, core_times]), 2, devices)
            wanted = [times, core_times, other[: times.shape[0]], other[times.shape[0] :]]
        halves = owners == 2
        if halves:
            blocks += shared
        else:
            mine = 0
            for bit in range(owners.bit_length() - 1):
                mine = 2 * mine + ((group >> bit) & 1)
            shared = jnp.take(jnp.stack(shared), jnp.arange(owners) ^ mine, axis=0)
            blocks.append(jnp.swapaxes(shared, 0, 1).reshape(count, rows, 2 * width))
        firsts.append((first, halves))
        first += count
    parts = select(blocks, firsts, wanted, slices, rows)
    sink_parts = [parts[0]] + [swap(parts[flip], flip, devices) for flip in range(1, 4)]
    src_parts = [parts[4]] + [swap(parts[4 + flip], flip, devices) for flip in range(1, 4)]
    return pair_blocks(peram, sink_parts, src_parts)


def solution(mesh):
    in_specs = (
        P("groups", None, None, None, "sink"),
        P("groups"),
        P(("groups", "sink"), None, None, None),
        P(("groups", "sink"), None),
    )
    out_specs = P(("groups", "sink"), None, None, None)
    return jax.shard_map(shards, mesh=mesh, in_specs=in_specs, out_specs=out_specs, check_vma=False)
```

```python
import functools
import math

import jax
import jax.numpy as jnp
from jax import lax
from jax.experimental import pallas as pl
from jax.experimental.pallas import tpu as pltpu
from jax.sharding import PartitionSpec as P

BF16 = jnp.bfloat16
F32 = jnp.float32
NT_DIMS = (((1,), (1,)), ((), ()))
CHUNKS = (4, 4)
ARRIVALS = (1, 2, 5)


def dot_nt(left, right):
    return lax.dot_general(left, right, NT_DIMS, preferred_element_type=F32)


def elemental_kernel(devices, chunks, arrivals, momentum, eigvecs, *refs):
    outs = refs[:-3]
    vec, total, arrived = refs[-3:]
    count, _, colors, width, sites = vec.shape
    rows = width // 4

    def load(at):
        return pltpu.make_async_copy(eigvecs.at[at], vec.at[at], arrived.at[at])

    for at in range(count):
        load(at).start()
    device = lax.axis_index("sink")
    core = jnp.bitwise_and(device, 1)
    chip = jnp.bitwise_and(lax.shift_right_logical(device, 1), 1)
    local = lax.broadcasted_iota(jnp.int32, (1, sites), 1)
    extent = sites // 16
    turn = jnp.mod(momentum[0:1, 0:1] * device, devices).astype(F32) / devices
    second = momentum[0:1, 1:2] * lax.shift_right_logical(local, 4)
    turn = turn + jnp.mod(second, extent).astype(F32) / extent
    third = momentum[0:1, 2:3] * jnp.bitwise_and(local, 15)
    turn = turn + jnp.mod(third, 16).astype(F32) / 16.0
    theta = (2.0 * math.pi) * turn
    cosine = jnp.cos(theta)
    sine = jnp.sin(theta)
    waits = [start for start, many in arrivals for _ in range(many)]
    for at in range(count):
        for late in range(at, count):
            if waits[late] == at:
                load(late).wait()
        plain = []
        rotated = []
        for color in range(colors):
            low_re = vec[at, 0, color]
            low_im = vec[at, 1, color]
            vec_re = low_re.astype(F32)
            vec_im = low_im.astype(F32)
            rot_re = (cosine * vec_re + sine * vec_im).astype(BF16)
            rot_im = (cosine * vec_im - sine * vec_re).astype(BF16)
            plain.append(jnp.concatenate([low_re, low_im], axis=0))
            rotated.append(jnp.concatenate([rot_re, rot_im], axis=0))
        both = dot_nt(jnp.concatenate(plain, axis=1), jnp.concatenate(rotated, axis=1))
        real = both[:width, :width] + both[width:, width:]
        imag = both[:width, width:] - both[width:, :width]
        total[at] = jnp.concatenate([real, imag], axis=1)
    for side in range(2):

        @pl.when(core == side)
        def _():
            first = 0
            for chunk, many in enumerate(chunks):
                keep, send = outs[2 * chunk : 2 * chunk + 2]
                for at in range(many):
                    for pair in range(2):
                        slot = jnp.bitwise_xor(chip, pair)
                        mine = (2 * pair + side) * rows
                        other = (2 * pair + 1 - side) * rows
                        keep[slot, at] = total[first + at, mine : mine + rows]
                        send[slot, at] = total[first + at, other : other + rows].astype(BF16)
                first += many


def elementals(eigvecs, momentum, devices):
    slices, _, colors, width, sites = eigvecs.shape
    rows = width // 4
    chunks = [part * slices // 8 for part in CHUNKS]
    arrivals = [part * slices // 8 for part in ARRIVALS]
    arrivals = [(sum(arrivals[:at]), many) for at, many in enumerate(arrivals)]
    shapes = []
    for count in chunks:
        shapes += [
            jax.ShapeDtypeStruct((2, count, rows, 2 * width), F32),
            jax.ShapeDtypeStruct((2, count, rows, 2 * width), BF16),
        ]
    outs = pl.pallas_call(
        functools.partial(elemental_kernel, devices, chunks, arrivals),
        in_specs=[pl.BlockSpec(memory_space=pltpu.VMEM), pl.BlockSpec(memory_space=pl.ANY)],
        out_specs=[pl.BlockSpec(memory_space=pltpu.VMEM)] * len(shapes),
        scratch_shapes=[
            pltpu.VMEM((slices, 2, colors, width, sites), BF16),
            pltpu.VMEM((slices, width, 2 * width), F32),
            pltpu.SemaphoreType.DMA((slices,)),
        ],
        out_shape=shapes,
        compiler_params=pltpu.CompilerParams(vmem_limit_bytes=50 * 1024 * 1024),
        cost_estimate=pl.CostEstimate(
            flops=slices * 8 * colors * width * width * sites,
            bytes_accessed=slices * 2 * colors * width * sites * 2,
            transcendentals=0,
        ),
        name="partial_elementals",
    )(momentum, eigvecs)
    return [outs[at : at + 2] for at in range(0, len(outs), 2)]


def select_kernel(firsts, *refs):
    many = sum(2 if halves else 1 for _, halves in firsts)
    wanted = refs[:4]
    blocks = refs[4 : 4 + many]
    outs = refs[4 + many : 8 + many]
    held = refs[-1]
    rows = held.shape[1]
    upper = jnp.bitwise_and(lax.shift_right_logical(lax.axis_index("sink"), 2), 1)
    for side in range(2):

        @pl.when(upper == side)
        def _():
            at = 0
            for first, halves in firsts:
                for flip in range(2 if halves else 1):
                    block = blocks[at]
                    start = (side ^ flip) * (rows // 2) if halves else 0
                    held[first : first + block.shape[0], start : start + block.shape[1], :] = block[...]
                    at += 1

    for out, times in zip(outs, wanted):
        for pair in range(out.shape[0]):
            for side in range(2):
                out[pair, side] = held[jnp.max(times[pair : pair + 1, side : side + 1])]


def select(blocks, firsts, wanted, slices, rows):
    pairs = wanted[0].shape[0]
    both = blocks[0].shape[2]
    shape = jax.ShapeDtypeStruct((pairs, 2, rows, both), BF16)
    return pl.pallas_call(
        functools.partial(select_kernel, firsts),
        in_specs=[pl.BlockSpec(memory_space=pltpu.VMEM)] * (4 + len(blocks)),
        out_specs=[pl.BlockSpec(memory_space=pltpu.VMEM)] * 4,
        scratch_shapes=[pltpu.VMEM((slices, rows, both), BF16)],
        out_shape=[shape] * 4,
        compiler_params=pltpu.CompilerParams(vmem_limit_bytes=8 * 1024 * 1024),
        name="select_slices",
    )(*wanted, *blocks)


def left_rows(pair, parts, peram, left, mat):
    width = peram.shape[2] // 4
    rows = parts[0].shape[2]
    half = 2 * rows
    for at, part in enumerate(parts):
        band = slice(at * rows, (at + 1) * rows)
        lower = slice(half + at * rows, half + (at + 1) * rows)
        a_re = part[pair, 0, :, :width]
        a_im = part[pair, 0, :, width:]
        mat[band] = jnp.concatenate([a_re, -a_im], axis=1)
        mat[lower] = jnp.concatenate([a_im, a_re], axis=1)
    for a in range(4):
        band = slice((a + 2) % 4 * width, ((a + 2) % 4 + 1) * width)
        stacked = jnp.concatenate([peram[pair, 0, band], peram[pair, 1, band]], axis=0)
        both = jnp.dot(mat[...], stacked, preferred_element_type=F32)
        both = (both if a < 2 else -both).astype(BF16)
        left[pair, 0, a] = both[:half]
        left[pair, 1, a] = both[half:]


def near_kernel(own, by_core, peram, left, mat):
    for pair in range(peram.shape[0]):
        left_rows(pair, (own, by_core), peram, left, mat)


def block_kernel(own, by_core, by_pair, by_both, near, peram, out, far, mat, src_el, right_mat, block, stored):
    width = src_el.shape[0]
    window = right_mat.shape[1] // 2
    edge = 2 * width - window
    rows = width // 4
    place = jnp.bitwise_and(lax.axis_index("sink"), 3)
    starts = [pl.multiple_of(jnp.bitwise_xor(place, flip) * rows, rows) for flip in range(4)]

    def store(pair, a):
        band = pl.ds(a * width, width)
        return pltpu.make_async_copy(block.at[a], out.at[pair, :, band, :], stored.at[a])

    for pair in range(peram.shape[0]):
        left_rows(pair, (by_pair, by_both), peram, far, mat)
        for start, part in zip(starts, (own, by_core, by_pair, by_both)):
            src_el[pl.ds(start, rows), :] = part[pair, 1]
        e_re = src_el[:, :width]
        e_im = src_el[:, width:]
        pad = jnp.zeros((width, window - width), BF16)
        hole = jnp.zeros((window - width, 2 * window), BF16)
        even_re = jnp.concatenate([e_re, pad, e_im, pad], axis=1)
        even_im = jnp.concatenate([-e_im, pad, e_re, pad], axis=1)
        odd_re = jnp.concatenate([pad, e_re, pad, e_im], axis=1)
        odd_im = jnp.concatenate([pad, -e_im, pad, e_re], axis=1)
        right_mat[0] = jnp.concatenate([even_re, hole, even_im, hole], axis=0)
        right_mat[1] = jnp.concatenate([hole, odd_re, hole, odd_im], axis=0)
        for a in range(4):
            results = []
            for odd in range(2):
                windows = [slice(b * width - odd * (window - width), b * width - odd * (window - width) + window) for b in (2 + odd, odd)]
                y_re = jnp.concatenate([part[pair, 0, a, :, at] for at in windows for part in (near, far)], axis=0)
                y_im = jnp.concatenate([part[pair, 1, a, :, at] for at in windows for part in (near, far)], axis=0)
                results.append(dot_nt(jnp.concatenate([y_re, y_im], axis=1), right_mat[odd]))
            if pair > 0:
                store(pair - 1, a).wait()
            for half in range(2):
                for part in range(2):
                    lanes = slice(part * window, (part + 1) * window)
                    first = 2 * half * width
                    for flip, start in enumerate(starts):
                        band = slice(half * width + flip * rows, half * width + (flip + 1) * rows)
                        even = results[0][band, lanes]
                        odd = results[1][band, lanes]
                        row = jnp.concatenate([even[:, :edge], even[:, edge:] + odd[:, : window - edge], odd[:, window - edge :]], axis=1)
                        block[a, part, pl.ds(start, rows), first : first + 2 * width] = row.astype(BF16)
            store(pair, a).start()
    for a in range(4):
        store(peram.shape[0] - 1, a).wait()


def pair_blocks(peram, parts):
    pairs, _, full, _ = peram.shape
    width = full // 4
    window = -(-width // 128) * 128
    params = pltpu.CompilerParams(vmem_limit_bytes=16 * 1024 * 1024)
    cost = pl.CostEstimate(
        flops=pairs * 8 * full * full * width, bytes_accessed=pairs * 4 * full * full, transcendentals=0
    )
    half = jax.ShapeDtypeStruct((pairs, 2, 4, width // 2, full), BF16)
    in_vmem = pl.BlockSpec(memory_space=pltpu.VMEM)
    near = pl.pallas_call(
        near_kernel,
        in_specs=[in_vmem] * 3,
        out_specs=in_vmem,
        scratch_shapes=[pltpu.VMEM((width, 2 * width), BF16)],
        out_shape=half,
        compiler_params=params,
        cost_estimate=cost,
        name="left_near",
    )(*parts[:2], peram)
    return pl.pallas_call(
        block_kernel,
        in_specs=[in_vmem] * 6,
        out_specs=pl.BlockSpec(memory_space=pl.ANY),
        scratch_shapes=[
            pltpu.VMEM(half.shape, BF16),
            pltpu.VMEM((width, 2 * width), BF16),
            pltpu.VMEM((width, 2 * width), BF16),
            pltpu.VMEM((2, 2 * window, 2 * window), BF16),
            pltpu.VMEM((4, 2, width, full), BF16),
            pltpu.SemaphoreType.DMA((4,)),
        ],
        out_shape=jax.ShapeDtypeStruct(peram.shape, BF16),
        compiler_params=params,
        cost_estimate=cost,
        name="meson_blocks",
    )(*parts, near, peram)


def swap(value, flip, devices):
    return lax.ppermute(value, "sink", [(i, i ^ flip) for i in range(devices)])


def sum_near(keep, send, devices):
    over_core = keep + swap(send, 1, devices).astype(F32)
    return over_core[0] + swap(over_core[1].astype(BF16), 2, devices).astype(F32)


def sum_far(near, flip, group, devices):
    count, rows, both = near.shape
    if 8 * flip == devices:
        return [(near + swap(near.astype(BF16), 4 * flip, devices).astype(F32)).astype(BF16)]
    cut = near.reshape(count, 2, rows // 2, both)
    bit = jnp.bitwise_and(lax.shift_right_logical(group, flip.bit_length() - 1), 1)
    kept = lax.dynamic_index_in_dim(cut, bit, 1, keepdims=False)
    given = lax.dynamic_index_in_dim(cut, 1 - bit, 1, keepdims=False).astype(BF16)
    kept = kept + swap(given, 4 * flip, devices).astype(F32)
    blocks = sum_far(kept, 2 * flip, group, devices)
    if len(blocks) == 1:
        return blocks + [swap(blocks[0], 4 * flip, devices)]
    other = swap(jnp.stack(blocks), 4 * flip, devices)
    return [block for at in range(len(blocks)) for block in (blocks[at], other[at])]


def shards(eigvecs, momentum, peram, times):
    devices = lax.axis_size("sink")
    group = lax.shift_right_logical(lax.axis_index("sink"), 2)
    owners = devices // 8
    slices, _, _, width, _ = eigvecs.shape
    rows = width // 4
    momentum = momentum.reshape(1, 3)
    blocks = []
    firsts = []
    nears = [sum_near(keep, send, devices) for keep, send in elementals(eigvecs, momentum, devices)]
    first = 0
    for near in nears:
        count = near.shape[0]
        shared = sum_far(near, 1, group, devices)
        if first == 0:
            late_times, shared[0] = lax.optimization_barrier((times, shared[0]))
            core_times = swap(late_times, 1, devices)
            other = swap(jnp.concatenate([late_times, core_times]), 2, devices)
            wanted = [times, core_times, other[: times.shape[0]], other[times.shape[0] :]]
        halves = owners == 2
        if halves:
            blocks += shared
        else:
            mine = 0
            for bit in range(owners.bit_length() - 1):
                mine = 2 * mine + ((group >> bit) & 1)
            shared = jnp.take(jnp.stack(shared), jnp.arange(owners) ^ mine, axis=0)
            blocks.append(jnp.swapaxes(shared, 0, 1).reshape(count, rows, 2 * width))
        firsts.append((first, halves))
        first += count
    parts = select(blocks, firsts, wanted, slices, rows)
    parts = [parts[0]] + [swap(parts[flip], flip, devices) for flip in range(1, 4)]
    return pair_blocks(peram, parts)


def solution(mesh):
    in_specs = (
        P("groups", None, None, None, "sink"),
        P("groups"),
        P(("groups", "sink"), None, None, None),
        P(("groups", "sink"), None),
    )
    out_specs = P(("groups", "sink"), None, None, None)
    return jax.shard_map(shards, mesh=mesh, in_specs=in_specs, out_specs=out_specs, check_vma=False)
```

```python
import functools
import math

import jax
import jax.numpy as jnp
from jax import lax
from jax.experimental import pallas as pl
from jax.experimental.pallas import tpu as pltpu
from jax.sharding import PartitionSpec as P

BF16 = jnp.bfloat16
F32 = jnp.float32
NT_DIMS = (((1,), (1,)), ((), ()))
CHUNKS = (4, 4)
ARRIVALS = (1, 2, 5)


def dot_nt(left, right):
    return lax.dot_general(left, right, NT_DIMS, preferred_element_type=F32)


def elemental_kernel(devices, chunks, arrivals, momentum, eigvecs, *refs):
    outs = refs[:-3]
    vec, total, arrived = refs[-3:]
    count, _, colors, width, sites = vec.shape
    rows = width // 4

    def load(at):
        return pltpu.make_async_copy(eigvecs.at[at], vec.at[at], arrived.at[at])

    for at in range(count):
        load(at).start()
    device = lax.axis_index("sink")
    core = jnp.bitwise_and(device, 1)
    chip = jnp.bitwise_and(lax.shift_right_logical(device, 1), 1)
    local = lax.broadcasted_iota(jnp.int32, (1, sites), 1)
    extent = sites // 16
    turn = jnp.mod(momentum[0:1, 0:1] * device, devices).astype(F32) / devices
    second = momentum[0:1, 1:2] * lax.shift_right_logical(local, 4)
    turn = turn + jnp.mod(second, extent).astype(F32) / extent
    third = momentum[0:1, 2:3] * jnp.bitwise_and(local, 15)
    turn = turn + jnp.mod(third, 16).astype(F32) / 16.0
    theta = (2.0 * math.pi) * turn
    cosine = jnp.cos(theta)
    sine = jnp.sin(theta)
    waits = [start for start, many in arrivals for _ in range(many)]
    for at in range(count):
        for late in range(at, count):
            if waits[late] == at:
                load(late).wait()
        plain = []
        rotated = []
        for color in range(colors):
            low_re = vec[at, 0, color]
            low_im = vec[at, 1, color]
            vec_re = low_re.astype(F32)
            vec_im = low_im.astype(F32)
            rot_re = (cosine * vec_re + sine * vec_im).astype(BF16)
            rot_im = (cosine * vec_im - sine * vec_re).astype(BF16)
            plain.append(jnp.concatenate([low_re, low_im], axis=0))
            rotated.append(jnp.concatenate([rot_re, rot_im], axis=0))
        both = dot_nt(jnp.concatenate(plain, axis=1), jnp.concatenate(rotated, axis=1))
        real = both[:width, :width] + both[width:, width:]
        imag = both[:width, width:] - both[width:, :width]
        total[at] = jnp.concatenate([real, imag], axis=1)
    for side in range(2):

        @pl.when(core == side)
        def _():
            first = 0
            for chunk, many in enumerate(chunks):
                keep, send = outs[2 * chunk : 2 * chunk + 2]
                for at in range(many):
                    for pair in range(2):
                        slot = jnp.bitwise_xor(chip, pair)
                        mine = (2 * pair + side) * rows
                        other = (2 * pair + 1 - side) * rows
                        keep[slot, at] = total[first + at, mine : mine + rows]
                        send[slot, at] = total[first + at, other : other + rows].astype(BF16)
                first += many


def elementals(eigvecs, momentum, devices):
    slices, _, colors, width, sites = eigvecs.shape
    rows = width // 4
    chunks = [part * slices // 8 for part in CHUNKS]
    arrivals = [part * slices // 8 for part in ARRIVALS]
    arrivals = [(sum(arrivals[:at]), many) for at, many in enumerate(arrivals)]
    shapes = []
    for count in chunks:
        shapes += [
            jax.ShapeDtypeStruct((2, count, rows, 2 * width), F32),
            jax.ShapeDtypeStruct((2, count, rows, 2 * width), BF16),
        ]
    outs = pl.pallas_call(
        functools.partial(elemental_kernel, devices, chunks, arrivals),
        in_specs=[pl.BlockSpec(memory_space=pltpu.VMEM), pl.BlockSpec(memory_space=pl.ANY)],
        out_specs=[pl.BlockSpec(memory_space=pltpu.VMEM)] * len(shapes),
        scratch_shapes=[
            pltpu.VMEM((slices, 2, colors, width, sites), BF16),
            pltpu.VMEM((slices, width, 2 * width), F32),
            pltpu.SemaphoreType.DMA((slices,)),
        ],
        out_shape=shapes,
        compiler_params=pltpu.CompilerParams(vmem_limit_bytes=50 * 1024 * 1024),
        cost_estimate=pl.CostEstimate(
            flops=slices * 8 * colors * width * width * sites,
            bytes_accessed=slices * 2 * colors * width * sites * 2,
            transcendentals=0,
        ),
        name="partial_elementals",
    )(momentum, eigvecs)
    return [outs[at : at + 2] for at in range(0, len(outs), 2)]


def select_kernel(*refs):
    wanted = refs[:8]
    chunks = refs[8:-5]
    outs = refs[-5:-1]
    held = refs[-1]
    first = 0
    for chunk in chunks:
        held[first : first + chunk.shape[0]] = chunk[...]
        first += chunk.shape[0]
    for at, times in enumerate(wanted):
        out = outs[at // 2]
        for pair in range(out.shape[1]):
            for side in range(2):
                out[at % 2, pair, side] = held[jnp.max(times[pair : pair + 1, side : side + 1])]


def select(chunks, wanted, slices):
    pairs = wanted[0].shape[0]
    _, rows, both = chunks[0].shape
    in_vmem = pl.BlockSpec(memory_space=pltpu.VMEM)
    return pl.pallas_call(
        select_kernel,
        in_specs=[in_vmem] * (8 + len(chunks)),
        out_specs=[in_vmem] * 4,
        scratch_shapes=[pltpu.VMEM((slices, rows, both), BF16)],
        out_shape=[jax.ShapeDtypeStruct((2, pairs, 2, rows, both), BF16)] * 4,
        compiler_params=pltpu.CompilerParams(vmem_limit_bytes=8 * 1024 * 1024),
        name="select_slices",
    )(*wanted, *chunks)


def join_halves(parts, flips, quarters):
    rows = parts[0].shape[3]
    upper = jnp.bitwise_and(lax.shift_right_logical(lax.axis_index("sink"), 2), 1)
    for side in range(2):

        @pl.when(upper == side)
        def _():
            for at in range(len(flips)):
                for half in range(2):
                    part = parts[2 * at + (half ^ side)]
                    quarters[flips[at], :, :, half * rows : (half + 1) * rows, :] = part[0]


def left_rows(pair, quarters, flips, peram, left, mat):
    width = peram.shape[2] // 4
    rows = quarters.shape[3]
    half = 2 * rows
    for at, flip in enumerate(flips):
        band = slice(at * rows, (at + 1) * rows)
        lower = slice(half + at * rows, half + (at + 1) * rows)
        a_re = quarters[flip, pair, 0, :, :width]
        a_im = quarters[flip, pair, 0, :, width:]
        mat[band] = jnp.concatenate([a_re, -a_im], axis=1)
        mat[lower] = jnp.concatenate([a_im, a_re], axis=1)
    for a in range(4):
        band = slice((a + 2) % 4 * width, ((a + 2) % 4 + 1) * width)
        stacked = jnp.concatenate([peram[pair, 0, band], peram[pair, 1, band]], axis=0)
        both = jnp.dot(mat[...], stacked, preferred_element_type=F32)
        both = (both if a < 2 else -both).astype(BF16)
        left[pair, 0, a] = both[:half]
        left[pair, 1, a] = both[half:]


def near_kernel(own, by_z, by_core, by_z_core, peram, left, quarters, mat):
    join_halves((own, by_z, by_core, by_z_core), (0, 1), quarters)
    for pair in range(peram.shape[0]):
        left_rows(pair, quarters, (0, 1), peram, left, mat)


def block_kernel(*refs):
    parts = refs[:8]
    near, peram, out, far, quarters, mat, src_el, right_mat, block, stored = refs[8:]
    width = src_el.shape[0]
    window = right_mat.shape[1] // 2
    edge = 2 * width - window
    rows = width // 4
    place = jnp.bitwise_and(lax.axis_index("sink"), 3)
    starts = [pl.multiple_of(jnp.bitwise_xor(place, flip) * rows, rows) for flip in range(4)]

    def store(pair, a):
        band = pl.ds(a * width, width)
        return pltpu.make_async_copy(block.at[a], out.at[pair, :, band, :], stored.at[a])

    join_halves(parts, (0, 1, 2, 3), quarters)
    for pair in range(peram.shape[0]):
        left_rows(pair, quarters, (2, 3), peram, far, mat)
        for flip, start in enumerate(starts):
            src_el[pl.ds(start, rows), :] = quarters[flip, pair, 1]
        e_re = src_el[:, :width]
        e_im = src_el[:, width:]
        pad = jnp.zeros((width, window - width), BF16)
        hole = jnp.zeros((window - width, 2 * window), BF16)
        even_re = jnp.concatenate([e_re, pad, e_im, pad], axis=1)
        even_im = jnp.concatenate([-e_im, pad, e_re, pad], axis=1)
        odd_re = jnp.concatenate([pad, e_re, pad, e_im], axis=1)
        odd_im = jnp.concatenate([pad, -e_im, pad, e_re], axis=1)
        right_mat[0] = jnp.concatenate([even_re, hole, even_im, hole], axis=0)
        right_mat[1] = jnp.concatenate([hole, odd_re, hole, odd_im], axis=0)
        for a in range(4):
            results = []
            for odd in range(2):
                windows = [slice(b * width - odd * (window - width), b * width - odd * (window - width) + window) for b in (2 + odd, odd)]
                y_re = jnp.concatenate([part[pair, 0, a, :, at] for at in windows for part in (near, far)], axis=0)
                y_im = jnp.concatenate([part[pair, 1, a, :, at] for at in windows for part in (near, far)], axis=0)
                results.append(dot_nt(jnp.concatenate([y_re, y_im], axis=1), right_mat[odd]))
            if pair > 0:
                store(pair - 1, a).wait()
            for half in range(2):
                for part in range(2):
                    lanes = slice(part * window, (part + 1) * window)
                    first = 2 * half * width
                    for flip, start in enumerate(starts):
                        band = slice(half * width + flip * rows, half * width + (flip + 1) * rows)
                        even = results[0][band, lanes]
                        odd = results[1][band, lanes]
                        row = jnp.concatenate([even[:, :edge], even[:, edge:] + odd[:, : window - edge], odd[:, window - edge :]], axis=1)
                        block[a, part, pl.ds(start, rows), first : first + 2 * width] = row.astype(BF16)
            store(pair, a).start()
    for a in range(4):
        store(peram.shape[0] - 1, a).wait()


def pair_blocks(peram, parts):
    pairs, _, full, _ = peram.shape
    width = full // 4
    window = -(-width // 128) * 128
    params = pltpu.CompilerParams(vmem_limit_bytes=16 * 1024 * 1024)
    cost = pl.CostEstimate(
        flops=pairs * 8 * full * full * width, bytes_accessed=pairs * 4 * full * full, transcendentals=0
    )
    quarters = (4, pairs, 2, width // 4, 2 * width)
    half = jax.ShapeDtypeStruct((pairs, 2, 4, width // 2, full), BF16)
    in_vmem = pl.BlockSpec(memory_space=pltpu.VMEM)
    near = pl.pallas_call(
        near_kernel,
        in_specs=[in_vmem] * 5,
        out_specs=in_vmem,
        scratch_shapes=[pltpu.VMEM(quarters, BF16), pltpu.VMEM((width, 2 * width), BF16)],
        out_shape=half,
        compiler_params=params,
        cost_estimate=cost,
        name="left_near",
    )(*parts[:4], peram)
    return pl.pallas_call(
        block_kernel,
        in_specs=[in_vmem] * 10,
        out_specs=pl.BlockSpec(memory_space=pl.ANY),
        scratch_shapes=[
            pltpu.VMEM(half.shape, BF16),
            pltpu.VMEM(quarters, BF16),
            pltpu.VMEM((width, 2 * width), BF16),
            pltpu.VMEM((width, 2 * width), BF16),
            pltpu.VMEM((2, 2 * window, 2 * window), BF16),
            pltpu.VMEM((4, 2, width, full), BF16),
            pltpu.SemaphoreType.DMA((4,)),
        ],
        out_shape=jax.ShapeDtypeStruct(peram.shape, BF16),
        compiler_params=params,
        cost_estimate=cost,
        name="meson_blocks",
    )(*parts, near, peram)


def swap(value, flip, devices):
    return lax.ppermute(value, "sink", [(i, i ^ flip) for i in range(devices)])


def with_times(rows, times):
    both = rows.shape[-1]
    known = jnp.concatenate([time.reshape(-1) for time in times]).astype(BF16)
    known = jnp.broadcast_to(jnp.pad(known, (0, both - known.shape[0])), (8, both))
    return jnp.concatenate([rows.reshape(-1, both), known])


def without_times(got, shape, many, times_shape):
    rows = math.prod(shape[:-1])
    times = got[rows, : many * math.prod(times_shape)].astype(jnp.int32).reshape(many, *times_shape)
    return got[:rows].reshape(shape), [times[at] for at in range(many)]


def sum_near(keep, send, devices, times=None):
    if times is None:
        over_core = keep + swap(send, 1, devices).astype(F32)
        given = over_core[1].astype(BF16)
        return over_core[0] + swap(given, 2, devices).astype(F32), None
    got, other = without_times(swap(with_times(send, [times]), 1, devices), send.shape, 1, times.shape)
    over_core = keep + got.astype(F32)
    given = over_core[1].astype(BF16)
    times = [times] + other
    got = swap(with_times(given, times), 2, devices)
    got, other = without_times(got, given.shape, 2, times[0].shape)
    return over_core[0] + got.astype(F32), times + other


def cut_rows(near, flip, group, devices, times=None):
    count, rows, both = near.shape
    cut = near.reshape(count, 2, rows // 2, both)
    bit = jnp.bitwise_and(lax.shift_right_logical(group, flip.bit_length() - 1), 1)
    kept = lax.dynamic_index_in_dim(cut, bit, 1, keepdims=False)
    given = lax.dynamic_index_in_dim(cut, 1 - bit, 1, keepdims=False).astype(BF16)
    if times is None:
        return kept + swap(given, 4 * flip, devices).astype(F32), None
    got = swap(with_times(given, times), 4 * flip, devices)
    got, other = without_times(got, given.shape, len(times), times[0].shape)
    return kept + got.astype(F32), times + other


def sum_rest(near, flip, group, devices):
    if 8 * flip == devices:
        return (near + swap(near.astype(BF16), 4 * flip, devices).astype(F32)).astype(BF16)
    kept, _ = cut_rows(near, flip, group, devices)
    mine = sum_rest(kept, 2 * flip, group, devices)
    other = swap(mine, 4 * flip, devices)
    bit = jnp.bitwise_and(lax.shift_right_logical(group, flip.bit_length() - 1), 1)
    return jnp.where(bit == 0, jnp.concatenate([mine, other], axis=1), jnp.concatenate([other, mine], axis=1))


def shards(eigvecs, momentum, peram, times):
    devices = lax.axis_size("sink")
    group = lax.shift_right_logical(lax.axis_index("sink"), 2)
    early, late = elementals(eigvecs, momentum.reshape(1, 3), devices)
    early, _ = sum_near(*early, devices)
    late, wanted = sum_near(*late, devices, times)
    early, _ = cut_rows(early, 1, group, devices)
    late, wanted = cut_rows(late, 1, group, devices, wanted)
    early = sum_rest(early, 2, group, devices)
    late = sum_rest(late, 2, group, devices)
    chips = select([early, late], wanted, eigvecs.shape[0])
    got = {0: chips[0]}
    for flip in (4, 6, 2):
        got[flip] = swap(chips[flip // 2], flip, devices)
    over = {flip: swap(value[1:], 1, devices) for flip, value in got.items()}
    return pair_blocks(peram, [got[0], got[4], over[0], over[4], got[2], got[6], over[2], over[6]])


def solution(mesh):
    in_specs = (
        P("groups", None, None, None, "sink"),
        P("groups"),
        P(("groups", "sink"), None, None, None),
        P(("groups", "sink"), None),
    )
    out_specs = P(("groups", "sink"), None, None, None)
    return jax.shard_map(shards, mesh=mesh, in_specs=in_specs, out_specs=out_specs, check_vma=False)
```

```python
import functools
import math

import jax
import jax.numpy as jnp
from jax import lax
from jax.experimental import pallas as pl
from jax.experimental.pallas import tpu as pltpu
from jax.sharding import PartitionSpec as P

BF16 = jnp.bfloat16
F32 = jnp.float32
NT_DIMS = (((1,), (1,)), ((), ()))
CHUNKS = (4, 4)
ARRIVALS = (1, 2, 5)


def dot_nt(left, right):
    return lax.dot_general(left, right, NT_DIMS, preferred_element_type=F32)


def elemental_kernel(devices, chunks, arrivals, momentum, eigvecs, *refs):
    outs = refs[:-3]
    vec, total, arrived = refs[-3:]
    count, _, colors, width, sites = vec.shape
    rows = width // 4

    def load(at):
        return pltpu.make_async_copy(eigvecs.at[at], vec.at[at], arrived.at[at])

    for at in range(count):
        load(at).start()
    device = lax.axis_index("sink")
    core = jnp.bitwise_and(device, 1)
    chip = jnp.bitwise_and(lax.shift_right_logical(device, 1), 1)
    local = lax.broadcasted_iota(jnp.int32, (1, sites), 1)
    extent = sites // 16
    turn = jnp.mod(momentum[0:1, 0:1] * device, devices).astype(F32) / devices
    second = momentum[0:1, 1:2] * lax.shift_right_logical(local, 4)
    turn = turn + jnp.mod(second, extent).astype(F32) / extent
    third = momentum[0:1, 2:3] * jnp.bitwise_and(local, 15)
    turn = turn + jnp.mod(third, 16).astype(F32) / 16.0
    theta = (2.0 * math.pi) * turn
    cosine = jnp.cos(theta)
    sine = jnp.sin(theta)
    waits = [start for start, many in arrivals for _ in range(many)]
    for at in range(count):
        for late in range(at, count):
            if waits[late] == at:
                load(late).wait()
        plain = []
        rotated = []
        for color in range(colors):
            low_re = vec[at, 0, color]
            low_im = vec[at, 1, color]
            vec_re = low_re.astype(F32)
            vec_im = low_im.astype(F32)
            rot_re = (cosine * vec_re + sine * vec_im).astype(BF16)
            rot_im = (cosine * vec_im - sine * vec_re).astype(BF16)
            plain.append(jnp.concatenate([low_re, low_im], axis=0))
            rotated.append(jnp.concatenate([rot_re, rot_im], axis=0))
        both = dot_nt(jnp.concatenate(plain, axis=1), jnp.concatenate(rotated, axis=1))
        real = both[:width, :width] + both[width:, width:]
        imag = both[:width, width:] - both[width:, :width]
        total[at] = jnp.concatenate([real, imag], axis=1)
    for side in range(2):

        @pl.when(core == side)
        def _():
            first = 0
            for chunk, many in enumerate(chunks):
                keep, send = outs[2 * chunk : 2 * chunk + 2]
                for at in range(many):
                    for pair in range(2):
                        slot = jnp.bitwise_xor(chip, pair)
                        mine = (2 * pair + side) * rows
                        other = (2 * pair + 1 - side) * rows
                        keep[slot, at] = total[first + at, mine : mine + rows]
                        send[slot, at] = total[first + at, other : other + rows].astype(BF16)
                first += many


def elementals(eigvecs, momentum, devices):
    slices, _, colors, width, sites = eigvecs.shape
    rows = width // 4
    chunks = [part * slices // 8 for part in CHUNKS]
    arrivals = [part * slices // 8 for part in ARRIVALS]
    arrivals = [(sum(arrivals[:at]), many) for at, many in enumerate(arrivals)]
    shapes = []
    for count in chunks:
        shapes += [
            jax.ShapeDtypeStruct((2, count, rows, 2 * width), F32),
            jax.ShapeDtypeStruct((2, count, rows, 2 * width), BF16),
        ]
    outs = pl.pallas_call(
        functools.partial(elemental_kernel, devices, chunks, arrivals),
        in_specs=[pl.BlockSpec(memory_space=pltpu.VMEM), pl.BlockSpec(memory_space=pl.ANY)],
        out_specs=[pl.BlockSpec(memory_space=pltpu.VMEM)] * len(shapes),
        scratch_shapes=[
            pltpu.VMEM((slices, 2, colors, width, sites), BF16),
            pltpu.VMEM((slices, width, 2 * width), F32),
            pltpu.SemaphoreType.DMA((slices,)),
        ],
        out_shape=shapes,
        compiler_params=pltpu.CompilerParams(vmem_limit_bytes=50 * 1024 * 1024),
        cost_estimate=pl.CostEstimate(
            flops=slices * 8 * colors * width * width * sites,
            bytes_accessed=slices * 2 * colors * width * sites * 2,
            transcendentals=0,
        ),
        name="partial_elementals",
    )(momentum, eigvecs)
    return [outs[at : at + 2] for at in range(0, len(outs), 2)]


def select_kernel(*refs):
    wanted = refs[:8]
    chunks = refs[8:-5]
    outs = refs[-5:-1]
    held = refs[-1]
    first = 0
    for chunk in chunks:
        held[first : first + chunk.shape[0]] = chunk[...]
        first += chunk.shape[0]
    for at, times in enumerate(wanted):
        out = outs[at // 2]
        for pair in range(out.shape[1]):
            for side in range(2):
                out[at % 2, pair, side] = held[jnp.max(times[pair : pair + 1, side : side + 1])]


def select(chunks, wanted, slices):
    pairs = wanted[0].shape[0]
    _, rows, both = chunks[0].shape
    in_vmem = pl.BlockSpec(memory_space=pltpu.VMEM)
    return pl.pallas_call(
        select_kernel,
        in_specs=[in_vmem] * (8 + len(chunks)),
        out_specs=[in_vmem] * 4,
        scratch_shapes=[pltpu.VMEM((slices, rows, both), BF16)],
        out_shape=[jax.ShapeDtypeStruct((2, pairs, 2, rows, both), BF16)] * 4,
        compiler_params=pltpu.CompilerParams(vmem_limit_bytes=8 * 1024 * 1024),
        name="select_slices",
    )(*wanted, *chunks)


def join_halves(parts, flips, quarters):
    rows = parts[0].shape[3]
    upper = jnp.bitwise_and(lax.shift_right_logical(lax.axis_index("sink"), 2), 1)
    for side in range(2):

        @pl.when(upper == side)
        def _():
            for at in range(len(flips)):
                for half in range(2):
                    part = parts[2 * at + (half ^ side)]
                    quarters[flips[at], :, :, half * rows : (half + 1) * rows, :] = part[0]


def left_rows(pair, quarters, flips, peram, left, mat):
    width = peram.shape[2] // 4
    rows = quarters.shape[3]
    half = 2 * rows
    for at, flip in enumerate(flips):
        band = slice(at * rows, (at + 1) * rows)
        lower = slice(half + at * rows, half + (at + 1) * rows)
        a_re = quarters[flip, pair, 0, :, :width]
        a_im = quarters[flip, pair, 0, :, width:]
        mat[band] = jnp.concatenate([a_re, -a_im], axis=1)
        mat[lower] = jnp.concatenate([a_im, a_re], axis=1)
    for a in range(4):
        band = slice((a + 2) % 4 * width, ((a + 2) % 4 + 1) * width)
        stacked = jnp.concatenate([peram[pair, 0, band], peram[pair, 1, band]], axis=0)
        both = jnp.dot(mat[...], stacked, preferred_element_type=F32)
        both = (both if a < 2 else -both).astype(BF16)
        left[pair, 0, a] = both[:half]
        left[pair, 1, a] = both[half:]


def across_kernel(by_both, by_x, by_both_core, by_x_core, peram, left, quarters, mat):
    join_halves((by_x, by_both, by_x_core, by_both_core), (2, 3), quarters)
    for pair in range(peram.shape[0]):
        left_rows(pair, quarters, (2, 3), peram, left, mat)


def block_kernel(*refs):
    parts = [refs[at] for at in (6, 2, 7, 5, 1, 0, 4, 3)]
    far, peram, out, near, quarters, mat, src_el, right_mat, block, stored = refs[8:]
    width = src_el.shape[0]
    window = right_mat.shape[1] // 2
    edge = 2 * width - window
    rows = width // 4
    place = jnp.bitwise_and(lax.axis_index("sink"), 3)
    starts = [pl.multiple_of(jnp.bitwise_xor(place, flip) * rows, rows) for flip in range(4)]

    def store(pair, a):
        band = pl.ds(a * width, width)
        return pltpu.make_async_copy(block.at[a], out.at[pair, :, band, :], stored.at[a])

    join_halves(parts, (0, 1, 2, 3), quarters)
    for pair in range(peram.shape[0]):
        left_rows(pair, quarters, (0, 1), peram, near, mat)
        for flip, start in enumerate(starts):
            src_el[pl.ds(start, rows), :] = quarters[flip, pair, 1]
        e_re = src_el[:, :width]
        e_im = src_el[:, width:]
        pad = jnp.zeros((width, window - width), BF16)
        hole = jnp.zeros((window - width, 2 * window), BF16)
        even_re = jnp.concatenate([e_re, pad, e_im, pad], axis=1)
        even_im = jnp.concatenate([-e_im, pad, e_re, pad], axis=1)
        odd_re = jnp.concatenate([pad, e_re, pad, e_im], axis=1)
        odd_im = jnp.concatenate([pad, -e_im, pad, e_re], axis=1)
        right_mat[0] = jnp.concatenate([even_re, hole, even_im, hole], axis=0)
        right_mat[1] = jnp.concatenate([hole, odd_re, hole, odd_im], axis=0)
        for a in range(4):
            results = []
            for odd in range(2):
                windows = [slice(b * width - odd * (window - width), b * width - odd * (window - width) + window) for b in (2 + odd, odd)]
                y_re = jnp.concatenate([part[pair, 0, a, :, at] for at in windows for part in (near, far)], axis=0)
                y_im = jnp.concatenate([part[pair, 1, a, :, at] for at in windows for part in (near, far)], axis=0)
                results.append(dot_nt(jnp.concatenate([y_re, y_im], axis=1), right_mat[odd]))
            if pair > 0:
                store(pair - 1, a).wait()
            for half in range(2):
                for part in range(2):
                    lanes = slice(part * window, (part + 1) * window)
                    first = 2 * half * width
                    for flip, start in enumerate(starts):
                        band = slice(half * width + flip * rows, half * width + (flip + 1) * rows)
                        even = results[0][band, lanes]
                        odd = results[1][band, lanes]
                        row = jnp.concatenate([even[:, :edge], even[:, edge:] + odd[:, : window - edge], odd[:, window - edge :]], axis=1)
                        block[a, part, pl.ds(start, rows), first : first + 2 * width] = row.astype(BF16)
            store(pair, a).start()
    for a in range(4):
        store(peram.shape[0] - 1, a).wait()


def pair_blocks(peram, parts):
    pairs, _, full, _ = peram.shape
    width = full // 4
    window = -(-width // 128) * 128
    params = pltpu.CompilerParams(vmem_limit_bytes=16 * 1024 * 1024)
    cost = pl.CostEstimate(
        flops=pairs * 8 * full * full * width, bytes_accessed=pairs * 4 * full * full, transcendentals=0
    )
    quarters = (4, pairs, 2, width // 4, 2 * width)
    half = jax.ShapeDtypeStruct((pairs, 2, 4, width // 2, full), BF16)
    in_vmem = pl.BlockSpec(memory_space=pltpu.VMEM)
    far = pl.pallas_call(
        across_kernel,
        in_specs=[in_vmem] * 5,
        out_specs=in_vmem,
        scratch_shapes=[pltpu.VMEM(quarters, BF16), pltpu.VMEM((width, 2 * width), BF16)],
        out_shape=half,
        compiler_params=params,
        cost_estimate=cost,
        name="left_across",
    )(*[parts[at] for at in (5, 4, 7, 6)], peram)
    return pl.pallas_call(
        block_kernel,
        in_specs=[in_vmem] * 10,
        out_specs=pl.BlockSpec(memory_space=pl.ANY),
        scratch_shapes=[
            pltpu.VMEM(half.shape, BF16),
            pltpu.VMEM(quarters, BF16),
            pltpu.VMEM((width, 2 * width), BF16),
            pltpu.VMEM((width, 2 * width), BF16),
            pltpu.VMEM((2, 2 * window, 2 * window), BF16),
            pltpu.VMEM((4, 2, width, full), BF16),
            pltpu.SemaphoreType.DMA((4,)),
        ],
        out_shape=jax.ShapeDtypeStruct(peram.shape, BF16),
        compiler_params=params,
        cost_estimate=cost,
        name="meson_blocks",
    )(*[parts[at] for at in (5, 4, 1, 7, 6, 3, 0, 2)], far, peram)


def swap(value, flip, devices):
    return lax.ppermute(value, "sink", [(i, i ^ flip) for i in range(devices)])


def with_times(rows, times):
    both = rows.shape[-1]
    known = jnp.concatenate([time.reshape(-1) for time in times]).astype(BF16)
    known = jnp.broadcast_to(jnp.pad(known, (0, both - known.shape[0])), (8, both))
    return jnp.concatenate([rows.reshape(-1, both), known])


def without_times(got, shape, many, times_shape):
    rows = math.prod(shape[:-1])
    times = got[rows, : many * math.prod(times_shape)].astype(jnp.int32).reshape(many, *times_shape)
    return got[:rows].reshape(shape), [times[at] for at in range(many)]


def sum_near(keep, send, devices, times=None):
    if times is None:
        over_core = keep + swap(send, 1, devices).astype(F32)
        given = over_core[1].astype(BF16)
        return over_core[0] + swap(given, 2, devices).astype(F32), None
    got, other = without_times(swap(with_times(send, [times]), 1, devices), send.shape, 1, times.shape)
    over_core = keep + got.astype(F32)
    given = over_core[1].astype(BF16)
    times = [times] + other
    got = swap(with_times(given, times), 2, devices)
    got, other = without_times(got, given.shape, 2, times[0].shape)
    return over_core[0] + got.astype(F32), times + other


def cut_rows(near, flip, group, devices, times=None):
    count, rows, both = near.shape
    cut = near.reshape(count, 2, rows // 2, both)
    bit = jnp.bitwise_and(lax.shift_right_logical(group, flip.bit_length() - 1), 1)
    kept = lax.dynamic_index_in_dim(cut, bit, 1, keepdims=False)
    given = lax.dynamic_index_in_dim(cut, 1 - bit, 1, keepdims=False).astype(BF16)
    if times is None:
        return kept + swap(given, 4 * flip, devices).astype(F32), None
    got = swap(with_times(given, times), 4 * flip, devices)
    got, other = without_times(got, given.shape, len(times), times[0].shape)
    return kept + got.astype(F32), times + other


def sum_rest(near, flip, group, devices):
    if 8 * flip == devices:
        return (near + swap(near.astype(BF16), 4 * flip, devices).astype(F32)).astype(BF16)
    kept, _ = cut_rows(near, flip, group, devices)
    mine = sum_rest(kept, 2 * flip, group, devices)
    other = swap(mine, 4 * flip, devices)
    bit = jnp.bitwise_and(lax.shift_right_logical(group, flip.bit_length() - 1), 1)
    return jnp.where(bit == 0, jnp.concatenate([mine, other], axis=1), jnp.concatenate([other, mine], axis=1))


def shards(eigvecs, momentum, peram, times):
    devices = lax.axis_size("sink")
    group = lax.shift_right_logical(lax.axis_index("sink"), 2)
    early, late = elementals(eigvecs, momentum.reshape(1, 3), devices)
    early, _ = sum_near(*early, devices)
    late, wanted = sum_near(*late, devices, times)
    early, _ = cut_rows(early, 1, group, devices)
    late, wanted = cut_rows(late, 1, group, devices, wanted)
    early = sum_rest(early, 2, group, devices)
    late = sum_rest(late, 2, group, devices)
    chips = select([early, late], wanted, eigvecs.shape[0])
    got = {0: chips[0]}
    for flip in (4, 6, 2):
        got[flip] = swap(chips[flip // 2], flip, devices)
    over = {flip: swap(value[1:], 1, devices) for flip, value in got.items()}
    return pair_blocks(peram, [got[0], got[4], over[0], over[4], got[2], got[6], over[2], over[6]])


def solution(mesh):
    in_specs = (
        P("groups", None, None, None, "sink"),
        P("groups"),
        P(("groups", "sink"), None, None, None),
        P(("groups", "sink"), None),
    )
    out_specs = P(("groups", "sink"), None, None, None)
    return jax.shard_map(shards, mesh=mesh, in_specs=in_specs, out_specs=out_specs, check_vma=False)
```

```python
import functools
import math

import jax
import jax.numpy as jnp
from jax import lax
from jax.experimental import pallas as pl
from jax.experimental.pallas import tpu as pltpu
from jax.sharding import PartitionSpec as P

BF16 = jnp.bfloat16
F32 = jnp.float32
NT_DIMS = (((1,), (1,)), ((), ()))
CHUNKS = (4, 4)
ARRIVALS = (1, 2, 5)


def dot_nt(left, right):
    return lax.dot_general(left, right, NT_DIMS, preferred_element_type=F32)


def elemental_kernel(devices, chunks, arrivals, momentum, eigvecs, *refs):
    outs = refs[:-3]
    vec, total, arrived = refs[-3:]
    count, _, colors, width, sites = vec.shape
    rows = width // 4

    def load(at):
        return pltpu.make_async_copy(eigvecs.at[at], vec.at[at], arrived.at[at])

    for at in range(count):
        load(at).start()
    device = lax.axis_index("sink")
    core = jnp.bitwise_and(device, 1)
    chip = jnp.bitwise_and(lax.shift_right_logical(device, 1), 1)
    local = lax.broadcasted_iota(jnp.int32, (1, sites), 1)
    extent = sites // 16
    turn = jnp.mod(momentum[0:1, 0:1] * device, devices).astype(F32) / devices
    second = momentum[0:1, 1:2] * lax.shift_right_logical(local, 4)
    turn = turn + jnp.mod(second, extent).astype(F32) / extent
    third = momentum[0:1, 2:3] * jnp.bitwise_and(local, 15)
    turn = turn + jnp.mod(third, 16).astype(F32) / 16.0
    theta = (2.0 * math.pi) * turn
    cosine = jnp.cos(theta)
    sine = jnp.sin(theta)
    waits = [start for start, many in arrivals for _ in range(many)]
    for at in range(count):
        for late in range(at, count):
            if waits[late] == at:
                load(late).wait()
        plain = []
        rotated = []
        for color in range(colors):
            low_re = vec[at, 0, color]
            low_im = vec[at, 1, color]
            vec_re = low_re.astype(F32)
            vec_im = low_im.astype(F32)
            rot_re = (cosine * vec_re + sine * vec_im).astype(BF16)
            rot_im = (cosine * vec_im - sine * vec_re).astype(BF16)
            plain.append(jnp.concatenate([low_re, low_im], axis=0))
            rotated.append(jnp.concatenate([rot_re, rot_im], axis=0))
        both = dot_nt(jnp.concatenate(plain, axis=1), jnp.concatenate(rotated, axis=1))
        real = both[:width, :width] + both[width:, width:]
        imag = both[:width, width:] - both[width:, :width]
        total[at] = jnp.concatenate([real, imag], axis=1)
    for side in range(2):

        @pl.when(core == side)
        def _():
            first = 0
            for chunk, many in enumerate(chunks):
                keep, send = outs[2 * chunk : 2 * chunk + 2]
                for at in range(many):
                    for pair in range(2):
                        slot = jnp.bitwise_xor(chip, pair)
                        mine = (2 * pair + side) * rows
                        other = (2 * pair + 1 - side) * rows
                        keep[slot, at] = total[first + at, mine : mine + rows]
                        send[slot, at] = total[first + at, other : other + rows].astype(BF16)
                first += many


def elementals(eigvecs, momentum, devices):
    slices, _, colors, width, sites = eigvecs.shape
    rows = width // 4
    chunks = [part * slices // 8 for part in CHUNKS]
    arrivals = [part * slices // 8 for part in ARRIVALS]
    arrivals = [(sum(arrivals[:at]), many) for at, many in enumerate(arrivals)]
    shapes = []
    for count in chunks:
        shapes += [
            jax.ShapeDtypeStruct((2, count, rows, 2 * width), F32),
            jax.ShapeDtypeStruct((2, count, rows, 2 * width), BF16),
        ]
    outs = pl.pallas_call(
        functools.partial(elemental_kernel, devices, chunks, arrivals),
        in_specs=[pl.BlockSpec(memory_space=pltpu.VMEM), pl.BlockSpec(memory_space=pl.ANY)],
        out_specs=[pl.BlockSpec(memory_space=pltpu.VMEM)] * len(shapes),
        scratch_shapes=[
            pltpu.VMEM((slices, 2, colors, width, sites), BF16),
            pltpu.VMEM((slices, width, 2 * width), F32),
            pltpu.SemaphoreType.DMA((slices,)),
        ],
        out_shape=shapes,
        compiler_params=pltpu.CompilerParams(vmem_limit_bytes=50 * 1024 * 1024),
        cost_estimate=pl.CostEstimate(
            flops=slices * 8 * colors * width * width * sites,
            bytes_accessed=slices * 2 * colors * width * sites * 2,
            transcendentals=0,
        ),
        name="partial_elementals",
    )(momentum, eigvecs)
    return [outs[at : at + 2] for at in range(0, len(outs), 2)]


def select_kernel(*refs):
    wanted = refs[:8]
    chunks = refs[8:-5]
    outs = refs[-5:-1]
    held = refs[-1]
    first = 0
    for chunk in chunks:
        held[first : first + chunk.shape[0]] = chunk[...]
        first += chunk.shape[0]
    for at, times in enumerate(wanted):
        out = outs[at // 2]
        for pair in range(out.shape[1]):
            for side in range(2):
                out[at % 2, pair, side] = held[jnp.max(times[pair : pair + 1, side : side + 1])]


def select(chunks, wanted, slices):
    pairs = wanted[0].shape[0]
    _, rows, both = chunks[0].shape
    in_vmem = pl.BlockSpec(memory_space=pltpu.VMEM)
    return pl.pallas_call(
        select_kernel,
        in_specs=[in_vmem] * (8 + len(chunks)),
        out_specs=[in_vmem] * 4,
        scratch_shapes=[pltpu.VMEM((slices, rows, both), BF16)],
        out_shape=[jax.ShapeDtypeStruct((2, pairs, 2, rows, both), BF16)] * 4,
        compiler_params=pltpu.CompilerParams(vmem_limit_bytes=8 * 1024 * 1024),
        name="select_slices",
    )(*wanted, *chunks)


def join_halves(parts, flips, quarters):
    rows = parts[0].shape[3]
    upper = jnp.bitwise_and(lax.shift_right_logical(lax.axis_index("sink"), 2), 1)
    for side in range(2):

        @pl.when(upper == side)
        def _():
            for at in range(len(flips)):
                for half in range(2):
                    part = parts[2 * at + (half ^ side)]
                    quarters[flips[at], :, :, half * rows : (half + 1) * rows, :] = part[0]


def left_rows(pair, quarters, flips, peram, left, mat):
    width = peram.shape[2] // 4
    rows = quarters.shape[3]
    half = len(flips) * rows
    for at, flip in enumerate(flips):
        band = slice(at * rows, (at + 1) * rows)
        lower = slice(half + at * rows, half + (at + 1) * rows)
        a_re = quarters[flip, pair, 0, :, :width]
        a_im = quarters[flip, pair, 0, :, width:]
        mat[band] = jnp.concatenate([a_re, -a_im], axis=1)
        mat[lower] = jnp.concatenate([a_im, a_re], axis=1)
    for a in range(4):
        band = slice((a + 2) % 4 * width, ((a + 2) % 4 + 1) * width)
        stacked = jnp.concatenate([peram[pair, 0, band], peram[pair, 1, band]], axis=0)
        both = jnp.dot(mat[...], stacked, preferred_element_type=F32)
        both = (both if a < 2 else -both).astype(BF16)
        left[pair, 0, a] = both[:half]
        left[pair, 1, a] = both[half:]


def across_kernel(by_both, by_x, peram, left, quarters, mat):
    join_halves((by_x, by_both), (2,), quarters)
    for pair in range(peram.shape[0]):
        left_rows(pair, quarters, (2,), peram, left, mat)


def block_kernel(*refs):
    parts = [refs[at] for at in (6, 2, 7, 5, 1, 0, 4, 3)]
    far, peram, out, near, quarters, mat, src_el, right_mat, block, stored = refs[8:]
    width = src_el.shape[0]
    window = right_mat.shape[1] // 2
    edge = 2 * width - window
    rows = width // 4
    place = jnp.bitwise_and(lax.axis_index("sink"), 3)
    starts = [pl.multiple_of(jnp.bitwise_xor(place, flip) * rows, rows) for flip in range(4)]

    def store(pair, a):
        band = pl.ds(a * width, width)
        return pltpu.make_async_copy(block.at[a], out.at[pair, :, band, :], stored.at[a])

    join_halves(parts, (0, 1, 2, 3), quarters)
    for pair in range(peram.shape[0]):
        left_rows(pair, quarters, (0, 1, 3), peram, near, mat)
        for flip, start in enumerate(starts):
            src_el[pl.ds(start, rows), :] = quarters[flip, pair, 1]
        e_re = src_el[:, :width]
        e_im = src_el[:, width:]
        pad = jnp.zeros((width, window - width), BF16)
        hole = jnp.zeros((window - width, 2 * window), BF16)
        even_re = jnp.concatenate([e_re, pad, e_im, pad], axis=1)
        even_im = jnp.concatenate([-e_im, pad, e_re, pad], axis=1)
        odd_re = jnp.concatenate([pad, e_re, pad, e_im], axis=1)
        odd_im = jnp.concatenate([pad, -e_im, pad, e_re], axis=1)
        right_mat[0] = jnp.concatenate([even_re, hole, even_im, hole], axis=0)
        right_mat[1] = jnp.concatenate([hole, odd_re, hole, odd_im], axis=0)
        for a in range(4):
            results = []
            for odd in range(2):
                windows = [slice(b * width - odd * (window - width), b * width - odd * (window - width) + window) for b in (2 + odd, odd)]
                y_re = jnp.concatenate([part[pair, 0, a, :, at] for at in windows for part in (near, far)], axis=0)
                y_im = jnp.concatenate([part[pair, 1, a, :, at] for at in windows for part in (near, far)], axis=0)
                results.append(dot_nt(jnp.concatenate([y_re, y_im], axis=1), right_mat[odd]))
            if pair > 0:
                store(pair - 1, a).wait()
            for half in range(2):
                for part in range(2):
                    lanes = slice(part * window, (part + 1) * window)
                    first = 2 * half * width
                    for at, flip in enumerate((0, 1, 3, 2)):
                        start = starts[flip]
                        band = slice(half * width + at * rows, half * width + (at + 1) * rows)
                        even = results[0][band, lanes]
                        odd = results[1][band, lanes]
                        row = jnp.concatenate([even[:, :edge], even[:, edge:] + odd[:, : window - edge], odd[:, window - edge :]], axis=1)
                        block[a, part, pl.ds(start, rows), first : first + 2 * width] = row.astype(BF16)
            store(pair, a).start()
    for a in range(4):
        store(peram.shape[0] - 1, a).wait()


def pair_blocks(peram, parts):
    pairs, _, full, _ = peram.shape
    width = full // 4
    window = -(-width // 128) * 128
    params = pltpu.CompilerParams(vmem_limit_bytes=16 * 1024 * 1024)
    cost = pl.CostEstimate(
        flops=pairs * 8 * full * full * width, bytes_accessed=pairs * 4 * full * full, transcendentals=0
    )
    quarters = (4, pairs, 2, width // 4, 2 * width)
    rows = width // 4
    one = jax.ShapeDtypeStruct((pairs, 2, 4, rows, full), BF16)
    in_vmem = pl.BlockSpec(memory_space=pltpu.VMEM)
    far = pl.pallas_call(
        across_kernel,
        in_specs=[in_vmem] * 3,
        out_specs=in_vmem,
        scratch_shapes=[pltpu.VMEM(quarters, BF16), pltpu.VMEM((2 * rows, 2 * width), BF16)],
        out_shape=one,
        compiler_params=params,
        cost_estimate=cost,
        name="left_across",
    )(*[parts[at] for at in (5, 4)], peram)
    return pl.pallas_call(
        block_kernel,
        in_specs=[in_vmem] * 10,
        out_specs=pl.BlockSpec(memory_space=pl.ANY),
        scratch_shapes=[
            pltpu.VMEM((pairs, 2, 4, 3 * rows, full), BF16),
            pltpu.VMEM(quarters, BF16),
            pltpu.VMEM((6 * rows, 2 * width), BF16),
            pltpu.VMEM((width, 2 * width), BF16),
            pltpu.VMEM((2, 2 * window, 2 * window), BF16),
            pltpu.VMEM((4, 2, width, full), BF16),
            pltpu.SemaphoreType.DMA((4,)),
        ],
        out_shape=jax.ShapeDtypeStruct(peram.shape, BF16),
        compiler_params=params,
        cost_estimate=cost,
        name="meson_blocks",
    )(*[parts[at] for at in (5, 4, 1, 7, 6, 3, 0, 2)], far, peram)


def swap(value, flip, devices):
    return lax.ppermute(value, "sink", [(i, i ^ flip) for i in range(devices)])


def with_times(rows, times):
    both = rows.shape[-1]
    known = jnp.concatenate([time.reshape(-1) for time in times]).astype(BF16)
    known = jnp.broadcast_to(jnp.pad(known, (0, both - known.shape[0])), (8, both))
    return jnp.concatenate([rows.reshape(-1, both), known])


def without_times(got, shape, many, times_shape):
    rows = math.prod(shape[:-1])
    times = got[rows, : many * math.prod(times_shape)].astype(jnp.int32).reshape(many, *times_shape)
    return got[:rows].reshape(shape), [times[at] for at in range(many)]


def sum_near(keep, send, devices, times=None):
    if times is None:
        over_core = keep + swap(send, 1, devices).astype(F32)
        given = over_core[1].astype(BF16)
        return over_core[0] + swap(given, 2, devices).astype(F32), None
    got, other = without_times(swap(with_times(send, [times]), 1, devices), send.shape, 1, times.shape)
    over_core = keep + got.astype(F32)
    given = over_core[1].astype(BF16)
    times = [times] + other
    got = swap(with_times(given, times), 2, devices)
    got, other = without_times(got, given.shape, 2, times[0].shape)
    return over_core[0] + got.astype(F32), times + other


def cut_rows(near, flip, group, devices, times=None):
    count, rows, both = near.shape
    cut = near.reshape(count, 2, rows // 2, both)
    bit = jnp.bitwise_and(lax.shift_right_logical(group, flip.bit_length() - 1), 1)
    kept = lax.dynamic_index_in_dim(cut, bit, 1, keepdims=False)
    given = lax.dynamic_index_in_dim(cut, 1 - bit, 1, keepdims=False).astype(BF16)
    if times is None:
        return kept + swap(given, 4 * flip, devices).astype(F32), None
    got = swap(with_times(given, times), 4 * flip, devices)
    got, other = without_times(got, given.shape, len(times), times[0].shape)
    return kept + got.astype(F32), times + other


def sum_rest(near, flip, group, devices):
    if 8 * flip == devices:
        return (near + swap(near.astype(BF16), 4 * flip, devices).astype(F32)).astype(BF16)
    kept, _ = cut_rows(near, flip, group, devices)
    mine = sum_rest(kept, 2 * flip, group, devices)
    other = swap(mine, 4 * flip, devices)
    bit = jnp.bitwise_and(lax.shift_right_logical(group, flip.bit_length() - 1), 1)
    return jnp.where(bit == 0, jnp.concatenate([mine, other], axis=1), jnp.concatenate([other, mine], axis=1))


def shards(eigvecs, momentum, peram, times):
    devices = lax.axis_size("sink")
    group = lax.shift_right_logical(lax.axis_index("sink"), 2)
    early, late = elementals(eigvecs, momentum.reshape(1, 3), devices)
    early, _ = sum_near(*early, devices)
    late, wanted = sum_near(*late, devices, times)
    early, _ = cut_rows(early, 1, group, devices)
    late, wanted = cut_rows(late, 1, group, devices, wanted)
    early = sum_rest(early, 2, group, devices)
    late = sum_rest(late, 2, group, devices)
    chips = select([early, late], wanted, eigvecs.shape[0])
    got = {0: chips[0]}
    for flip in (4, 6, 2):
        got[flip] = swap(chips[flip // 2], flip, devices)
    over = {flip: swap(value[1:], 1, devices) for flip, value in got.items()}
    return pair_blocks(peram, [got[0], got[4], over[0], over[4], got[2], got[6], over[2], over[6]])


def solution(mesh):
    in_specs = (
        P("groups", None, None, None, "sink"),
        P("groups"),
        P(("groups", "sink"), None, None, None),
        P(("groups", "sink"), None),
    )
    out_specs = P(("groups", "sink"), None, None, None)
    return jax.shard_map(shards, mesh=mesh, in_specs=in_specs, out_specs=out_specs, check_vma=False)
```

```python
import functools
import math

import jax
import jax.numpy as jnp
from jax import lax
from jax.experimental import pallas as pl
from jax.experimental.pallas import tpu as pltpu
from jax.sharding import PartitionSpec as P

BF16 = jnp.bfloat16
F32 = jnp.float32
NT_DIMS = (((1,), (1,)), ((), ()))
CHUNKS = (4, 4)
ARRIVALS = (1, 2, 5)


def dot_nt(left, right):
    return lax.dot_general(left, right, NT_DIMS, preferred_element_type=F32)


def elemental_kernel(devices, chunks, arrivals, momentum, eigvecs, *refs):
    outs = refs[:-3]
    vec, total, arrived = refs[-3:]
    count, _, colors, width, sites = vec.shape
    rows = width // 4

    def load(at):
        return pltpu.make_async_copy(eigvecs.at[at], vec.at[at], arrived.at[at])

    for at in range(count):
        load(at).start(priority=0 if at == 0 else 1)
    device = lax.axis_index("sink")
    core = jnp.bitwise_and(device, 1)
    chip = jnp.bitwise_and(lax.shift_right_logical(device, 1), 1)
    local = lax.broadcasted_iota(jnp.int32, (1, sites), 1)
    extent = sites // 16
    turn = jnp.mod(momentum[0:1, 0:1] * device, devices).astype(F32) / devices
    second = momentum[0:1, 1:2] * lax.shift_right_logical(local, 4)
    turn = turn + jnp.mod(second, extent).astype(F32) / extent
    third = momentum[0:1, 2:3] * jnp.bitwise_and(local, 15)
    turn = turn + jnp.mod(third, 16).astype(F32) / 16.0
    theta = (2.0 * math.pi) * turn
    cosine = jnp.cos(theta)
    sine = jnp.sin(theta)
    waits = [start for start, many in arrivals for _ in range(many)]
    for at in range(count):
        for late in range(at, count):
            if waits[late] == at:
                load(late).wait()
        plain = []
        rotated = []
        for color in range(colors):
            low_re = vec[at, 0, color]
            low_im = vec[at, 1, color]
            vec_re = low_re.astype(F32)
            vec_im = low_im.astype(F32)
            rot_re = (cosine * vec_re + sine * vec_im).astype(BF16)
            rot_im = (cosine * vec_im - sine * vec_re).astype(BF16)
            plain.append(jnp.concatenate([low_re, low_im], axis=0))
            rotated.append(jnp.concatenate([rot_re, rot_im], axis=0))
        both = dot_nt(jnp.concatenate(plain, axis=1), jnp.concatenate(rotated, axis=1))
        real = both[:width, :width] + both[width:, width:]
        imag = both[:width, width:] - both[width:, :width]
        total[at] = jnp.concatenate([real, imag], axis=1)
    for side in range(2):

        @pl.when(core == side)
        def _():
            first = 0
            for chunk, many in enumerate(chunks):
                keep, send = outs[2 * chunk : 2 * chunk + 2]
                for at in range(many):
                    for pair in range(2):
                        slot = jnp.bitwise_xor(chip, pair)
                        mine = (2 * pair + side) * rows
                        other = (2 * pair + 1 - side) * rows
                        keep[slot, at] = total[first + at, mine : mine + rows]
                        send[slot, at] = total[first + at, other : other + rows].astype(BF16)
                first += many


def elementals(eigvecs, momentum, devices):
    slices, _, colors, width, sites = eigvecs.shape
    rows = width // 4
    chunks = [part * slices // 8 for part in CHUNKS]
    arrivals = [part * slices // 8 for part in ARRIVALS]
    arrivals = [(sum(arrivals[:at]), many) for at, many in enumerate(arrivals)]
    shapes = []
    for count in chunks:
        shapes += [
            jax.ShapeDtypeStruct((2, count, rows, 2 * width), F32),
            jax.ShapeDtypeStruct((2, count, rows, 2 * width), BF16),
        ]
    outs = pl.pallas_call(
        functools.partial(elemental_kernel, devices, chunks, arrivals),
        in_specs=[pl.BlockSpec(memory_space=pltpu.VMEM), pl.BlockSpec(memory_space=pl.ANY)],
        out_specs=[pl.BlockSpec(memory_space=pltpu.VMEM)] * len(shapes),
        scratch_shapes=[
            pltpu.VMEM((slices, 2, colors, width, sites), BF16),
            pltpu.VMEM((slices, width, 2 * width), F32),
            pltpu.SemaphoreType.DMA((slices,)),
        ],
        out_shape=shapes,
        compiler_params=pltpu.CompilerParams(vmem_limit_bytes=50 * 1024 * 1024),
        cost_estimate=pl.CostEstimate(
            flops=slices * 8 * colors * width * width * sites,
            bytes_accessed=slices * 2 * colors * width * sites * 2,
            transcendentals=0,
        ),
        name="partial_elementals",
    )(momentum, eigvecs)
    return [outs[at : at + 2] for at in range(0, len(outs), 2)]


def select_kernel(*refs):
    wanted = refs[:8]
    chunks = refs[8:-5]
    outs = refs[-5:-1]
    held = refs[-1]
    first = 0
    for chunk in chunks:
        held[first : first + chunk.shape[0]] = chunk[...]
        first += chunk.shape[0]
    for at, times in enumerate(wanted):
        out = outs[at // 2]
        for pair in range(out.shape[1]):
            for side in range(2):
                out[at % 2, pair, side] = held[jnp.max(times[pair : pair + 1, side : side + 1])]


def select(chunks, wanted, slices):
    pairs = wanted[0].shape[0]
    _, rows, both = chunks[0].shape
    in_vmem = pl.BlockSpec(memory_space=pltpu.VMEM)
    return pl.pallas_call(
        select_kernel,
        in_specs=[in_vmem] * (8 + len(chunks)),
        out_specs=[in_vmem] * 4,
        scratch_shapes=[pltpu.VMEM((slices, rows, both), BF16)],
        out_shape=[jax.ShapeDtypeStruct((2, pairs, 2, rows, both), BF16)] * 4,
        compiler_params=pltpu.CompilerParams(vmem_limit_bytes=8 * 1024 * 1024),
        name="select_slices",
    )(*wanted, *chunks)


def join_halves(parts, flips, quarters):
    rows = parts[0].shape[3]
    upper = jnp.bitwise_and(lax.shift_right_logical(lax.axis_index("sink"), 2), 1)
    for side in range(2):

        @pl.when(upper == side)
        def _():
            for at in range(len(flips)):
                for half in range(2):
                    part = parts[2 * at + (half ^ side)]
                    quarters[flips[at], :, :, half * rows : (half + 1) * rows, :] = part[0]


def left_rows(pair, quarters, flips, peram, left, mat):
    width = peram.shape[2] // 4
    rows = quarters.shape[3]
    half = 2 * rows
    for at, flip in enumerate(flips):
        band = slice(at * rows, (at + 1) * rows)
        lower = slice(half + at * rows, half + (at + 1) * rows)
        a_re = quarters[flip, pair, 0, :, :width]
        a_im = quarters[flip, pair, 0, :, width:]
        mat[band] = jnp.concatenate([a_re, -a_im], axis=1)
        mat[lower] = jnp.concatenate([a_im, a_re], axis=1)
    for a in range(4):
        band = slice((a + 2) % 4 * width, ((a + 2) % 4 + 1) * width)
        stacked = jnp.concatenate([peram[pair, 0, band], peram[pair, 1, band]], axis=0)
        both = jnp.dot(mat[...], stacked, preferred_element_type=F32)
        both = (both if a < 2 else -both).astype(BF16)
        left[pair, 0, a] = both[:half]
        left[pair, 1, a] = both[half:]


def across_kernel(by_both, by_x, by_both_core, by_x_core, peram, left, quarters, mat):
    join_halves((by_x, by_both, by_x_core, by_both_core), (2, 3), quarters)
    for pair in range(peram.shape[0]):
        left_rows(pair, quarters, (2, 3), peram, left, mat)


def block_kernel(*refs):
    parts = [refs[at] for at in (6, 2, 7, 5, 1, 0, 4, 3)]
    far, peram, out, near, quarters, mat, src_el, right_mat, block, stored = refs[8:]
    width = src_el.shape[0]
    window = right_mat.shape[1] // 2
    edge = 2 * width - window
    rows = width // 4
    place = jnp.bitwise_and(lax.axis_index("sink"), 3)
    starts = [pl.multiple_of(jnp.bitwise_xor(place, flip) * rows, rows) for flip in range(4)]

    def store(pair, a):
        band = pl.ds(a * width, width)
        return pltpu.make_async_copy(block.at[a], out.at[pair, :, band, :], stored.at[a])

    join_halves(parts, (0, 1, 2, 3), quarters)
    for pair in range(peram.shape[0]):
        left_rows(pair, quarters, (0, 1), peram, near, mat)
        for flip, start in enumerate(starts):
            src_el[pl.ds(start, rows), :] = quarters[flip, pair, 1]
        e_re = src_el[:, :width]
        e_im = src_el[:, width:]
        pad = jnp.zeros((width, window - width), BF16)
        hole = jnp.zeros((window - width, 2 * window), BF16)
        even_re = jnp.concatenate([e_re, pad, e_im, pad], axis=1)
        even_im = jnp.concatenate([-e_im, pad, e_re, pad], axis=1)
        odd_re = jnp.concatenate([pad, e_re, pad, e_im], axis=1)
        odd_im = jnp.concatenate([pad, -e_im, pad, e_re], axis=1)
        right_mat[0] = jnp.concatenate([even_re, hole, even_im, hole], axis=0)
        right_mat[1] = jnp.concatenate([hole, odd_re, hole, odd_im], axis=0)
        for a in range(4):
            results = []
            for odd in range(2):
                windows = [slice(b * width - odd * (window - width), b * width - odd * (window - width) + window) for b in (2 + odd, odd)]
                y_re = jnp.concatenate([part[pair, 0, a, :, at] for at in windows for part in (near, far)], axis=0)
                y_im = jnp.concatenate([part[pair, 1, a, :, at] for at in windows for part in (near, far)], axis=0)
                results.append(dot_nt(jnp.concatenate([y_re, y_im], axis=1), right_mat[odd]))
            if pair > 0:
                store(pair - 1, a).wait()
            for half in range(2):
                for part in range(2):
                    lanes = slice(part * window, (part + 1) * window)
                    first = 2 * half * width
                    for flip, start in enumerate(starts):
                        band = slice(half * width + flip * rows, half * width + (flip + 1) * rows)
                        even = results[0][band, lanes]
                        odd = results[1][band, lanes]
                        row = jnp.concatenate([even[:, :edge], even[:, edge:] + odd[:, : window - edge], odd[:, window - edge :]], axis=1)
                        block[a, part, pl.ds(start, rows), first : first + 2 * width] = row.astype(BF16)
            store(pair, a).start()
    for a in range(4):
        store(peram.shape[0] - 1, a).wait()


def pair_blocks(peram, parts):
    pairs, _, full, _ = peram.shape
    width = full // 4
    window = -(-width // 128) * 128
    params = pltpu.CompilerParams(vmem_limit_bytes=16 * 1024 * 1024)
    cost = pl.CostEstimate(
        flops=pairs * 8 * full * full * width, bytes_accessed=pairs * 4 * full * full, transcendentals=0
    )
    quarters = (4, pairs, 2, width // 4, 2 * width)
    half = jax.ShapeDtypeStruct((pairs, 2, 4, width // 2, full), BF16)
    in_vmem = pl.BlockSpec(memory_space=pltpu.VMEM)
    far = pl.pallas_call(
        across_kernel,
        in_specs=[in_vmem] * 5,
        out_specs=in_vmem,
        scratch_shapes=[pltpu.VMEM(quarters, BF16), pltpu.VMEM((width, 2 * width), BF16)],
        out_shape=half,
        compiler_params=params,
        cost_estimate=cost,
        name="left_across",
    )(*[parts[at] for at in (5, 4, 7, 6)], peram)
    return pl.pallas_call(
        block_kernel,
        in_specs=[in_vmem] * 10,
        out_specs=pl.BlockSpec(memory_space=pl.ANY),
        scratch_shapes=[
            pltpu.VMEM(half.shape, BF16),
            pltpu.VMEM(quarters, BF16),
            pltpu.VMEM((width, 2 * width), BF16),
            pltpu.VMEM((width, 2 * width), BF16),
            pltpu.VMEM((2, 2 * window, 2 * window), BF16),
            pltpu.VMEM((4, 2, width, full), BF16),
            pltpu.SemaphoreType.DMA((4,)),
        ],
        out_shape=jax.ShapeDtypeStruct(peram.shape, BF16),
        compiler_params=params,
        cost_estimate=cost,
        name="meson_blocks",
    )(*[parts[at] for at in (5, 4, 1, 7, 6, 3, 0, 2)], far, peram)


def swap(value, flip, devices):
    return lax.ppermute(value, "sink", [(i, i ^ flip) for i in range(devices)])


def with_times(rows, times):
    both = rows.shape[-1]
    known = jnp.concatenate([time.reshape(-1) for time in times]).astype(BF16)
    known = jnp.broadcast_to(jnp.pad(known, (0, both - known.shape[0])), (8, both))
    return jnp.concatenate([rows.reshape(-1, both), known])


def without_times(got, shape, many, times_shape):
    rows = math.prod(shape[:-1])
    times = got[rows, : many * math.prod(times_shape)].astype(jnp.int32).reshape(many, *times_shape)
    return got[:rows].reshape(shape), [times[at] for at in range(many)]


def sum_near(keep, send, devices, times=None):
    if times is None:
        over_core = keep + swap(send, 1, devices).astype(F32)
        given = over_core[1].astype(BF16)
        return over_core[0] + swap(given, 2, devices).astype(F32), None
    got, other = without_times(swap(with_times(send, [times]), 1, devices), send.shape, 1, times.shape)
    over_core = keep + got.astype(F32)
    given = over_core[1].astype(BF16)
    times = [times] + other
    got = swap(with_times(given, times), 2, devices)
    got, other = without_times(got, given.shape, 2, times[0].shape)
    return over_core[0] + got.astype(F32), times + other


def cut_rows(near, flip, group, devices, times=None):
    count, rows, both = near.shape
    cut = near.reshape(count, 2, rows // 2, both)
    bit = jnp.bitwise_and(lax.shift_right_logical(group, flip.bit_length() - 1), 1)
    kept = lax.dynamic_index_in_dim(cut, bit, 1, keepdims=False)
    given = lax.dynamic_index_in_dim(cut, 1 - bit, 1, keepdims=False).astype(BF16)
    if times is None:
        return kept + swap(given, 4 * flip, devices).astype(F32), None
    got = swap(with_times(given, times), 4 * flip, devices)
    got, other = without_times(got, given.shape, len(times), times[0].shape)
    return kept + got.astype(F32), times + other


def sum_rest(near, flip, group, devices):
    if 8 * flip == devices:
        return (near + swap(near.astype(BF16), 4 * flip, devices).astype(F32)).astype(BF16)
    kept, _ = cut_rows(near, flip, group, devices)
    mine = sum_rest(kept, 2 * flip, group, devices)
    other = swap(mine, 4 * flip, devices)
    bit = jnp.bitwise_and(lax.shift_right_logical(group, flip.bit_length() - 1), 1)
    return jnp.where(bit == 0, jnp.concatenate([mine, other], axis=1), jnp.concatenate([other, mine], axis=1))


def shards(eigvecs, momentum, peram, times):
    devices = lax.axis_size("sink")
    group = lax.shift_right_logical(lax.axis_index("sink"), 2)
    early, late = elementals(eigvecs, momentum.reshape(1, 3), devices)
    early, _ = sum_near(*early, devices)
    late, wanted = sum_near(*late, devices, times)
    early, _ = cut_rows(early, 1, group, devices)
    late, wanted = cut_rows(late, 1, group, devices, wanted)
    early = sum_rest(early, 2, group, devices)
    late = sum_rest(late, 2, group, devices)
    chips = select([early, late], wanted, eigvecs.shape[0])
    got = {0: chips[0]}
    for flip in (4, 6, 2):
        got[flip] = swap(chips[flip // 2], flip, devices)
    over = {flip: swap(value[1:], 1, devices) for flip, value in got.items()}
    return pair_blocks(peram, [got[0], got[4], over[0], over[4], got[2], got[6], over[2], over[6]])


def solution(mesh):
    in_specs = (
        P("groups", None, None, None, "sink"),
        P("groups"),
        P(("groups", "sink"), None, None, None),
        P(("groups", "sink"), None),
    )
    out_specs = P(("groups", "sink"), None, None, None)
    return jax.shard_map(shards, mesh=mesh, in_specs=in_specs, out_specs=out_specs, check_vma=False)
```
